32 devices in a mesh: dp: 4 (over x, core), ctx: 4 (over z), tensor: 2 (over y).
Axes of the slice: x: 2, y: 2, z: 4, core: 2. Of those that a mesh axis runs over, the one named last changes fastest.
Arguments:
- hidden_in: bfloat16 [4, 1024, 1536], P('dp', 'ctx'), may hold values from -6 to 6
- doc_pos: int32 [4, 1024], P('dp', 'ctx'), may hold values from 0 to 1022, as said below
- mixer_gain: bfloat16 [1536], P(('dp', 'ctx')), may hold values from 0.25 to 1.75
- mixer_in: bfloat16 [3, 1536, 1536], P(None, ('dp', 'ctx'), 'tensor'), may hold values from -0.15625 to 0.15625
- conv_taps: bfloat16 [3, 1536], P(None, 'tensor'), may hold values from -3 to 3
- mixer_out: bfloat16 [1536, 1536], P('tensor', ('dp', 'ctx')), may hold values from -0.15625 to 0.15625
- feed_first: bfloat16 [1536], P(('dp', 'ctx')), may hold values from 0.25 to 1.75
- gate_first: bfloat16 [1536, 6912], P(('dp', 'ctx'), 'tensor'), may hold values from -0.15625 to 0.15625
- lift_first: bfloat16 [1536, 6912], P(('dp', 'ctx'), 'tensor'), may hold values from -0.15625 to 0.15625
- down_first: bfloat16 [6912, 1536], P('tensor', ('dp', 'ctx')), may hold values from -0.078125 to 0.078125
- attend_gain: bfloat16 [1536], P(('dp', 'ctx')), may hold values from 0.25 to 1.75
- query_proj: bfloat16 [1536, 1536], P(('dp', 'ctx'), 'tensor'), may hold values from -0.15625 to 0.15625
- key_proj: bfloat16 [1536, 512], P(('dp', 'ctx'), 'tensor'), may hold values from -0.15625 to 0.15625
- value_proj: bfloat16 [1536, 512], P(('dp', 'ctx'), 'tensor'), may hold values from -0.15625 to 0.15625
- query_gain: bfloat16 [64], replicated, may hold values from 0.25 to 1.75
- key_gain: bfloat16 [64], replicated, may hold values from 0.25 to 1.75
- attend_out: bfloat16 [1536, 1536], P('tensor', ('dp', 'ctx')), may hold values from -1.25 to 1.25
- feed_second: bfloat16 [1536], P(('dp', 'ctx')), may hold values from 0.25 to 1.75
- gate_second: bfloat16 [1536, 6912], P(('dp', 'ctx'), 'tensor'), may hold values from -0.15625 to 0.15625
- lift_second: bfloat16 [1536, 6912], P(('dp', 'ctx'), 'tensor'), may hold values from -0.15625 to 0.15625
- down_second: bfloat16 [6912, 1536], P('tensor', ('dp', 'ctx')), may hold values from -0.078125 to 0.078125
- output_grad: bfloat16 [4, 1024, 1536], P('dp', 'ctx'), may hold values from -6 to 6
Outputs:
- hidden_out: bfloat16 [4, 1024, 1536], P('dp', 'ctx')
- hidden_grad: bfloat16 [4, 1024, 1536], P('dp', 'ctx')
- mixer_gain_grad: float32 [1536], P(('dp', 'ctx'))
- mixer_in_grad: float32 [3, 1536, 1536], P(None, ('dp', 'ctx'), 'tensor')
- conv_taps_grad: float32 [3, 1536], P(None, 'tensor')
- mixer_out_grad: float32 [1536, 1536], P('tensor', ('dp', 'ctx'))
- feed_first_grad: float32 [1536], P(('dp', 'ctx'))
- gate_first_grad: float32 [1536, 6912], P(('dp', 'ctx'), 'tensor')
- lift_first_grad: float32 [1536, 6912], P(('dp', 'ctx'), 'tensor')
- down_first_grad: float32 [6912, 1536], P('tensor', ('dp', 'ctx'))
- attend_gain_grad: float32 [1536], P(('dp', 'ctx'))
- query_proj_grad: float32 [1536, 1536], P(('dp', 'ctx'), 'tensor')
- key_proj_grad: float32 [1536, 512], P(('dp', 'ctx'), 'tensor')
- value_proj_grad: float32 [1536, 512], P(('dp', 'ctx'), 'tensor')
- query_gain_grad: float32 [64], replicated
- key_gain_grad: float32 [64], replicated
- attend_out_grad: float32 [1536, 1536], P('tensor', ('dp', 'ctx'))
- feed_second_grad: float32 [1536], P(('dp', 'ctx'))
- gate_second_grad: float32 [1536, 6912], P(('dp', 'ctx'), 'tensor')
- lift_second_grad: float32 [1536, 6912], P(('dp', 'ctx'), 'tensor')
- down_second_grad: float32 [6912, 1536], P('tensor', ('dp', 'ctx'))
The draws below stay inside these ranges and needn't reach their ends.
Inputs may be any that keep to these rules, and one draw needn't show every extreme that they name: doc_pos[s, t] is t minus the first index of the contiguous document of sequence s that holds token t, so documents start where it is 0; token 0 starts one; every sequence holds one document that starts within its first 256 tokens and ends within its last 256; in one sequence that document runs from token 1 to the end.
All inputs are finite; a program needn't handle non-finite values.
Results may differ from the reference program's by a relative error of at most 0.025.
Values may be sent and summed in bfloat16 or wider, within the bound.
A program may use at most 832 MiB of HBM per device.

```python
import math
import jax
import jax.numpy as jnp
from jax import lax

D = 1536
H = 24
KV = 8
HD = 64
FF = 6912
TOK_DEV = 256
SEQS = 4
LENGTH = 1024


def draw_doc_pos(key, part):
    key = jax.random.fold_in(key, 11)
    sub_keys = jax.random.split(key, 5)
    index = jnp.arange(LENGTH, dtype=jnp.int32)[None, :]
    seq_index = jnp.arange(SEQS, dtype=jnp.int32)[:, None]
    chosen = jax.random.randint(sub_keys[4], (), 0, SEQS)
    long_start = jax.random.randint(sub_keys[0], (SEQS, 1), 1, TOK_DEV)
    long_end = LENGTH - jax.random.randint(sub_keys[1], (SEQS, 1), 0, TOK_DEV - 1)
    long_start = jnp.where(seq_index == chosen, 1, long_start)
    long_end = jnp.where(seq_index == chosen, LENGTH, long_end)
    exponents = jax.random.randint(sub_keys[2], (SEQS, LENGTH // TOK_DEV), 2, 10)
    exponents = jnp.repeat(exponents, TOK_DEV, axis=1)
    raw_bits = jax.random.randint(sub_keys[3], (SEQS, LENGTH), 0, 4096)
    random_start = raw_bits < jnp.right_shift(jnp.full_like(exponents, 4096), exponents)
    outside = (index < long_start) | (index >= long_end)
    start_flag = (index == 0) | (index == long_start) | (index == long_end) | outside & random_start
    last_start = lax.cummax(jnp.where(start_flag, index, 0), axis=1)
    return (index - last_start).astype(jnp.int32)


def block_scale(rng, dims, shards, smallest, high):
    def one(axis_at, blocks):
        draws = jax.random.uniform(jax.random.fold_in(jax.random.fold_in(rng, 6), axis_at), (blocks,), jnp.float32, smallest / len(shards), high / len(shards))
        return jnp.repeat(jnp.exp(draws), dims[axis_at] // blocks).reshape((-1,) + (1,) * (len(dims) - axis_at - 1))

    gain = one(*shards[0])
    for cut in shards[1:]:
        gain = gain * one(*cut)
    return gain


def bell_draw(own_key, extent, width, limit, cuts=(), held_as=jnp.bfloat16):
    values = jax.random.normal(own_key, extent, jnp.float32) * width
    if len(cuts) > 0:
        values = block_scale(own_key, extent, cuts, -0.22, 0.18) * values
    return jnp.clip(values, min=-limit, max=limit).astype(held_as)


def setup_inputs(seed: int = 0) -> dict:
    key_of = jax.random.split(jax.random.key(seed), 23)
    return {
        "hidden_in": bell_draw(key_of[0], (SEQS, LENGTH, D), 1.0, 6.0, ((0, 4), (1, 4))),
        "doc_pos": draw_doc_pos(jax.random.fold_in(key_of[22], 71), 0),
        "mixer_gain": jnp.clip(1.0 + 0.15 * jax.random.normal(key_of[2], (D,), jnp.float32), 0.25, 1.75).astype(jnp.bfloat16),
        "mixer_in": bell_draw(key_of[3], (3, D, D), D ** -0.5, 0.15625, ((1, 16), (2, 2))),
        "conv_taps": bell_draw(key_of[4], (3, D), 0.6, 3.0, ((1, 2),)),
        "mixer_out": bell_draw(key_of[5], (D, D), D ** -0.5, 0.15625, ((0, 2), (1, 16))),
        "feed_first": jnp.clip(1.0 + 0.15 * jax.random.normal(key_of[6], (D,), jnp.float32), 0.25, 1.75).astype(jnp.bfloat16),
        "gate_first": bell_draw(key_of[7], (D, FF), D ** -0.5, 0.15625, ((0, 16), (1, 2))),
        "lift_first": bell_draw(key_of[8], (D, FF), D ** -0.5, 0.15625, ((0, 16), (1, 2))),
        "down_first": bell_draw(key_of[9], (FF, D), FF ** -0.5, 0.078125, ((0, 2), (1, 16))),
        "attend_gain": jnp.clip(1.0 + 0.15 * jax.random.normal(key_of[10], (D,), jnp.float32), 0.25, 1.75).astype(jnp.bfloat16),
        "query_proj": bell_draw(key_of[11], (D, H * HD), D ** -0.5, 0.15625, ((0, 16), (1, 2))),
        "key_proj": bell_draw(key_of[12], (D, KV * HD), D ** -0.5, 0.15625, ((0, 16), (1, 2))),
        "value_proj": bell_draw(key_of[13], (D, KV * HD), D ** -0.5, 0.15625, ((0, 16), (1, 2))),
        "query_gain": jnp.clip(1.0 + 0.15 * jax.random.normal(key_of[14], (HD,), jnp.float32), 0.25, 1.75).astype(jnp.bfloat16),
        "key_gain": jnp.clip(1.0 + 0.15 * jax.random.normal(key_of[15], (HD,), jnp.float32), 0.25, 1.75).astype(jnp.bfloat16),
        "attend_out": bell_draw(key_of[16], (H * HD, D), (max(4, H * HD // 64)) ** -0.5, 1.25, ((0, 2), (1, 16))),
        "feed_second": jnp.clip(1.0 + 0.15 * jax.random.normal(key_of[17], (D,), jnp.float32), 0.25, 1.75).astype(jnp.bfloat16),
        "gate_second": bell_draw(key_of[18], (D, FF), D ** -0.5, 0.15625, ((0, 16), (1, 2))),
        "lift_second": bell_draw(key_of[19], (D, FF), D ** -0.5, 0.15625, ((0, 16), (1, 2))),
        "down_second": bell_draw(key_of[20], (FF, D), FF ** -0.5, 0.078125, ((0, 2), (1, 16))),
        "output_grad": bell_draw(key_of[21], (SEQS, LENGTH, D), 1.0, 6.0, ((0, 4), (1, 4))),
    }


@jax.custom_vjp
def low(v):
    return lax.optimization_barrier(v.astype(jnp.bfloat16)).astype(jnp.float32)

@jax.custom_vjp
def low_back(v):
    return v

def low_keep(v):
    return (low(v), None)

def low_pass(kept, grad):
    return (grad,)

def back_keep(v):
    return (v, None)

def back_low(kept, grad):
    return (low(grad),)
low.defvjp(low_keep, low_pass)
low_back.defvjp(back_keep, back_low)

def rms_scale(values):
    return lax.rsqrt(lax.optimization_barrier(jnp.mean(values * values, -1, keepdims=True)) + 1e-05)

def high_dot(left, right):
    return jnp.dot(left, right, precision=lax.Precision.HIGHEST)

def rotary_tables(positions):
    half_dim = HD // 2
    freqs = jnp.exp(-math.log(1000000.0) * 2.0 * jnp.arange(half_dim, dtype=jnp.float32) / HD)
    angles = positions.astype(jnp.float32)[:, None] * freqs[None, :]
    return (jnp.cos(angles), jnp.sin(angles))

def rotate(values, cosine, sine):
    half_dim = values.shape[-1] // 2
    first_half = values[..., :half_dim]
    second_half = values[..., half_dim:]
    cos_rows = cosine[:, None, :]
    sin_rows = sine[:, None, :]
    return jnp.concatenate([first_half * cos_rows - second_half * sin_rows, second_half * cos_rows + first_half * sin_rows], -1)

def feed_block(stream, norm_gain, gate_weight, lift_weight, down_weight):
    normed = low(stream * rms_scale(stream) * norm_gain)
    gate_out = low_back(high_dot(normed, gate_weight))
    lift_out = low_back(high_dot(normed, lift_weight))
    hidden = low(jax.nn.silu(gate_out) * lift_out)
    return stream + low_back(high_dot(hidden, down_weight))

def mixer_block(stream, positions, norm_gain, lift_in, conv_taps, lift_out):
    normed = low(stream * rms_scale(stream) * norm_gain)
    projected = low_back(jnp.einsum('td,kde->kte', normed, lift_in, precision=lax.Precision.HIGHEST))
    conv_src = low(projected[0] * projected[2])
    padded = jnp.concatenate([jnp.zeros((2, conv_src.shape[1]), jnp.float32), conv_src], 0)
    row_count = conv_src.shape[0]
    conv_sum = jnp.zeros_like(conv_src)
    for offset in range(3):
        in_doc = (positions >= offset).astype(jnp.float32)[:, None]
        conv_sum = conv_sum + conv_taps[offset] * padded[2 - offset:2 - offset + row_count] * in_doc
    gated = low(projected[1] * conv_sum)
    return stream + low_back(high_dot(gated, lift_out))

def attend_block(stream, positions, norm_gain, query_proj, key_proj, value_proj, query_gain, key_gain, attend_out):
    row_count = stream.shape[0]
    groups = H // KV
    normed = low(stream * rms_scale(stream) * norm_gain)
    queries = low_back(high_dot(normed, query_proj)).reshape(row_count, H, HD)
    keys = low_back(high_dot(normed, key_proj)).reshape(row_count, KV, HD)
    values = low_back(high_dot(normed, value_proj)).reshape(row_count, KV, HD)
    cosine, sine = rotary_tables(positions)
    query_rot = low(rotate(queries * rms_scale(queries) * query_gain, cosine, sine))
    key_rot = low(rotate(keys * rms_scale(keys) * key_gain, cosine, sine))
    value_low = low(values)
    block_rows = min(512, row_count)
    key_at = jnp.arange(row_count, dtype=jnp.int32)

    def one_block(start):
        query_block = lax.dynamic_slice_in_dim(query_rot, start, block_rows, 0).reshape(block_rows, KV, groups, HD)
        scores = jnp.einsum('tkgd,skd->kgts', query_block, key_rot, precision=lax.Precision.HIGHEST) / math.sqrt(HD)
        scores = low_back(scores)
        query_at = start + jnp.arange(block_rows, dtype=jnp.int32)
        query_from = query_at - lax.dynamic_slice_in_dim(positions, start, block_rows, 0)
        allowed = (key_at[None, :] <= query_at[:, None]) & (key_at[None, :] >= query_from[:, None])
        scores = jnp.where(allowed[None, None], scores, -1e+30)
        top_score = lax.optimization_barrier(jnp.max(scores, -1, keepdims=True))
        weights = jnp.exp(scores - top_score)
        probs = low(weights / lax.optimization_barrier(jnp.sum(weights, -1, keepdims=True)))
        context = jnp.einsum('kgts,skd->tkgd', probs, value_low, precision=lax.Precision.HIGHEST)
        return context.reshape(block_rows, H * HD)
    starts = jnp.arange(row_count // block_rows, dtype=jnp.int32) * block_rows
    context = lax.map(jax.checkpoint(one_block), starts).reshape(row_count, H * HD)
    context = low_back(low(context))
    return stream + low_back(high_dot(context, attend_out))

def forward(stream, positions, params):
    mixer_gain, mixer_in, conv_taps, mixer_out, feed_first, gate_first, lift_first, down_first, attend_gain, query_proj, key_proj, value_proj, query_gain, key_gain, attend_out, feed_second, gate_second, lift_second, down_second = params
    stream = mixer_block(stream, positions, mixer_gain, mixer_in, conv_taps, mixer_out)
    stream = feed_block(stream, feed_first, gate_first, lift_first, down_first)
    stream = attend_block(stream, positions, attend_gain, query_proj, key_proj, value_proj, query_gain, key_gain, attend_out)
    return feed_block(stream, feed_second, gate_second, lift_second, down_second)

def reference(hidden_in, doc_pos, mixer_gain, mixer_in, conv_taps, mixer_out, feed_first, gate_first, lift_first, down_first, attend_gain, query_proj, key_proj, value_proj, query_gain, key_gain, attend_out, feed_second, gate_second, lift_second, down_second, output_grad):
    params = tuple((weight.astype(jnp.float32) for weight in (mixer_gain, mixer_in, conv_taps, mixer_out, feed_first, gate_first, lift_first, down_first, attend_gain, query_proj, key_proj, value_proj, query_gain, key_gain, attend_out, feed_second, gate_second, lift_second, down_second)))
    zero_totals = tuple((jnp.zeros_like(weight) for weight in params))

    def per_sequence(totals, inputs):
        seq_in, seq_pos, seq_grad = inputs

        def apply_layers(stream, *weights):
            return forward(stream, seq_pos, weights)
        result, pullback = jax.vjp(apply_layers, seq_in.astype(jnp.float32), *params)
        grads = pullback(seq_grad.astype(jnp.float32))
        new_totals = tuple((total + grad for total, grad in zip(totals, grads[1:])))
        return (new_totals, (result.astype(jnp.bfloat16), grads[0].astype(jnp.bfloat16)))
    totals, (outputs, input_grads) = lax.scan(per_sequence, zero_totals, (hidden_in, doc_pos, output_grad))
    return (outputs, input_grads, totals[0], totals[1], totals[2], totals[3], totals[4], totals[5], totals[6], totals[7], totals[8], totals[9], totals[10], totals[11], totals[12], totals[13], totals[14], totals[15], totals[16], totals[17], totals[18])
```

```python
import functools
import math

import jax
import jax.numpy as jnp
from jax import lax
from jax.experimental import pallas as pl
from jax.experimental.pallas import tpu as pltpu
from jax.sharding import PartitionSpec as P

H = 24
KV = 8
HD = 64
GROUPS = H // KV
LANES = 128

epsilon = 1e-05
MESH = pl.DeviceIdType.MESH


def plane_place():
    dp = lax.axis_index("dp")
    ten = lax.axis_index("tensor")
    core = lax.rem(dp, 2)
    across = lax.rem(dp + 2, 4)
    twin = dp + 1 - 2 * core
    return dp, ten, core, across, twin


def greet(dp, ten, across, twin):
    barrier = pltpu.get_barrier_semaphore()
    pl.semaphore_signal(barrier, 1, device_id={"dp": across}, device_id_type=MESH)
    pl.semaphore_signal(barrier, 1, device_id={"tensor": 1 - ten}, device_id_type=MESH)
    pl.semaphore_signal(barrier, 1, device_id={"dp": twin}, device_id_type=MESH)
    pl.semaphore_wait(barrier, 3)


def remote(src, dst, send, recv, place):
    return pltpu.make_async_remote_copy(
        src_ref=src,
        dst_ref=dst,
        send_sem=send,
        recv_sem=recv,
        device_id=place,
        device_id_type=MESH,
    )


def gather_kernel(x_ref, o_ref, own_sem, send, recv):
    dp, ten, core, across, twin = plane_place()
    greet(dp, ten, across, twin)
    to_across = {"dp": across, "tensor": ten}
    to_side = {"dp": dp, "tensor": 1 - ten}
    to_twin = {"dp": twin, "tensor": ten}
    own = dp * 2 + ten
    first = (across * (1 - core) + dp * core) * 2 + ten * (1 - core) + (1 - ten) * core
    other = (dp * (1 - core) + across * core) * 2 + (1 - ten) * (1 - core) + ten * core
    onward = {
        "dp": dp * (1 - core) + across * core,
        "tensor": (1 - ten) * (1 - core) + ten * core,
    }
    far = across * 2 + 1 - ten

    def move(src, slot, number, place):
        copy = remote(src, o_ref.at[slot], send.at[number], recv.at[slot], place)
        copy.start()
        return copy

    copies = [
        move(x_ref, own, 0, to_across),
        move(x_ref, own, 1, to_side),
        move(x_ref, own, 2, to_twin),
    ]
    local = pltpu.make_async_copy(x_ref, o_ref.at[own], own_sem)
    local.start()

    def arrived(slot):
        remote(x_ref, o_ref.at[slot], send.at[0], recv.at[slot], to_twin).wait_recv()

    arrived(first)
    copies.append(move(o_ref.at[first], first, 3, onward))
    copies.append(move(o_ref.at[first], first, 4, to_twin))
    arrived(other)
    copies.append(move(o_ref.at[other], other, 5, to_twin))
    arrived(far)
    copies.append(move(o_ref.at[far], far, 6, to_twin))
    twin_across = lax.rem(twin + 2, 4)
    for there in (twin, twin_across):
        for side in range(2):
            arrived(there * 2 + side)
    local.wait()
    for copy in copies:
        copy.wait_send()


def plane_gather(block):
    rows, width = block.shape
    slots = lax.axis_size("dp") * lax.axis_size("tensor")
    gathered = pl.pallas_call(
        gather_kernel,
        out_shape=jax.ShapeDtypeStruct((slots, rows, width), block.dtype),
        in_specs=[pl.BlockSpec(memory_space=pltpu.VMEM)],
        out_specs=pl.BlockSpec(memory_space=pl.ANY),
        scratch_shapes=[
            pltpu.SemaphoreType.DMA,
            pltpu.SemaphoreType.DMA((7,)),
            pltpu.SemaphoreType.DMA((8,)),
        ],
        compiler_params=pltpu.CompilerParams(
            collective_id=1, has_side_effects=True, vmem_limit_bytes=16 << 20
        ),
    )(block)
    return gathered.reshape(slots * rows, width)


def scatter_kernel(p_ref, o_ref, mine, theirs, out_box, in_box, load, send, recv):
    dp, ten, core, across, twin = plane_place()
    greet(dp, ten, across, twin)
    twin_across = lax.rem(twin + 2, 4)
    to_twin = {"dp": twin, "tensor": ten}
    sides = (ten, 1 - ten, ten, 1 - ten)
    home = (dp, dp, across, across)
    away = (twin, twin, twin_across, twin_across)
    order = (3, 1, 2, 0)
    loads = {}
    gifts = {}
    for rel in order:
        gifts[rel] = remote(
            p_ref.at[away[rel] * 2 + sides[rel]],
            theirs.at[rel],
            send.at[rel],
            recv.at[rel],
            to_twin,
        )
        gifts[rel].start()
        loads[rel] = pltpu.make_async_copy(
            p_ref.at[home[rel] * 2 + sides[rel]], mine.at[rel], load.at[rel]
        )
        loads[rel].start()
    direct = 1 + core
    relayed = 2 - core
    to_direct = {
        "dp": dp * (1 - core) + across * core,
        "tensor": (1 - ten) * (1 - core) + ten * core,
    }
    to_relayed = {
        "dp": across * (1 - core) + dp * core,
        "tensor": ten * (1 - core) + (1 - ten) * core,
    }

    def total(rel):
        return mine[rel].astype(jnp.float32) + theirs[rel].astype(jnp.float32)

    def post(number, value, place):
        out_box[number] = value.astype(out_box.dtype)
        copy = remote(
            out_box.at[number], in_box.at[number], send.at[4 + number], recv.at[4 + number], place
        )
        copy.start()
        return copy

    loads[3].wait()
    gifts[3].wait_recv()
    relay = post(0, total(3), to_direct)
    for rel in (1, 2):
        loads[rel].wait()
        gifts[rel].wait_recv()
    straight = post(1, total(direct), to_direct)
    relay.wait_recv()
    bent = post(2, total(relayed) + in_box[0].astype(jnp.float32), to_relayed)
    loads[0].wait()
    gifts[0].wait_recv()
    partial = total(0)
    straight.wait_recv()
    partial = partial + in_box[1].astype(jnp.float32)
    bent.wait_recv()
    o_ref[...] = partial + in_box[2].astype(jnp.float32)
    for rel in order:
        gifts[rel].wait_send()
    for copy in (relay, straight, bent):
        copy.wait_send()


def plane_scatter(partial):
    slots = lax.axis_size("dp") * lax.axis_size("tensor")
    rows, width = partial.shape[0] // slots, partial.shape[1]
    block = (rows, width)
    return pl.pallas_call(
        scatter_kernel,
        out_shape=jax.ShapeDtypeStruct(block, jnp.float32),
        in_specs=[pl.BlockSpec(memory_space=pl.ANY)],
        out_specs=pl.BlockSpec(memory_space=pltpu.VMEM),
        scratch_shapes=[
            pltpu.VMEM((4,) + block, jnp.bfloat16),
            pltpu.VMEM((4,) + block, jnp.bfloat16),
            pltpu.VMEM((3,) + block, jnp.bfloat16),
            pltpu.VMEM((3,) + block, jnp.bfloat16),
            pltpu.SemaphoreType.DMA((4,)),
            pltpu.SemaphoreType.DMA((7,)),
            pltpu.SemaphoreType.DMA((7,)),
        ],
        compiler_params=pltpu.CompilerParams(
            collective_id=2, has_side_effects=True, vmem_limit_bytes=24 << 20
        ),
    )(partial.astype(jnp.bfloat16).reshape((slots,) + block))


def swap_kernel(x_ref, o_ref, own_sem, send, recv):
    dp = lax.axis_index("dp")
    ten = lax.axis_index("tensor")
    barrier = pltpu.get_barrier_semaphore()
    for step in (1, 2, 3):
        pl.semaphore_signal(
            barrier,
            1,
            device_id={"dp": lax.rem(dp + step, 4), "tensor": ten},
            device_id_type=MESH,
        )
    pl.semaphore_wait(barrier, 3)
    copies = []
    for step in (2, 1, 3):
        there = lax.rem(dp + step, 4)
        copy = remote(
            x_ref.at[there],
            o_ref.at[dp],
            send.at[step],
            recv.at[step],
            {"dp": there, "tensor": ten},
        )
        copy.start()
        copies.append(copy)
    local = pltpu.make_async_copy(x_ref.at[dp], o_ref.at[dp], own_sem)
    local.start()
    for copy in copies:
        copy.wait()
    local.wait()


def swap_blocks(blocks, number):
    return pl.pallas_call(
        swap_kernel,
        out_shape=jax.ShapeDtypeStruct(blocks.shape, blocks.dtype),
        in_specs=[pl.BlockSpec(memory_space=pltpu.VMEM)],
        out_specs=pl.BlockSpec(memory_space=pl.ANY),
        scratch_shapes=[
            pltpu.SemaphoreType.DMA,
            pltpu.SemaphoreType.DMA((4,)),
            pltpu.SemaphoreType.DMA((4,)),
        ],
        compiler_params=pltpu.CompilerParams(
            collective_id=number, has_side_effects=True, vmem_limit_bytes=16 << 20
        ),
    )(blocks)


def return_blocks(blocks):
    dp = lax.axis_index("dp")
    devices = range(lax.axis_size("dp"))
    parts = [lax.dynamic_index_in_dim(blocks, dp, 0, keepdims=False)]
    for flip in (1, 2, 3):
        sent = lax.dynamic_index_in_dim(blocks, dp ^ flip, 0, keepdims=False)
        parts.append(lax.ppermute(sent, "dp", [(i, i ^ flip) for i in devices]))
    ordered = [lax.select_n(dp, *(parts[j ^ i] for i in devices)) for j in devices]
    return jnp.stack(ordered, 1)


def from_all_dp(block):
    dp = lax.axis_index("dp")
    devices = range(lax.axis_size("dp"))
    parts = [block] + [
        lax.ppermute(block, "dp", [(i, i ^ flip) for i in devices]) for flip in (1, 2, 3)
    ]
    return jnp.concatenate([lax.select_n(dp, *(parts[j ^ i] for i in devices)) for j in devices], 0)


def after(values, *others):
    return lax.optimization_barrier((values,) + others)[0]


def small_sum_kernel(x_ref, o_ref, plane_box, plane_sum, line_box, send, recv, line_send, line_recv):
    dp, ten, ctx = (lax.axis_index(name) for name in ("dp", "tensor", "ctx"))
    dps, tens, ctxs = (lax.axis_size(name) for name in ("dp", "tensor", "ctx"))
    slots = dps * tens
    own = dp * tens + ten
    barrier = pltpu.get_barrier_semaphore()

    def plane_peer(step):
        slot = lax.rem(own + step, slots)
        return {"dp": slot // tens, "tensor": lax.rem(slot, tens), "ctx": ctx}

    def line_peer(step):
        return {"dp": dp, "tensor": ten, "ctx": lax.rem(ctx + step, ctxs)}

    for step in range(1, slots):
        pl.semaphore_signal(barrier, 1, device_id=plane_peer(step), device_id_type=MESH)
    for step in range(1, ctxs):
        pl.semaphore_signal(barrier, 1, device_id=line_peer(step), device_id_type=MESH)
    pl.semaphore_wait(barrier, slots + ctxs - 2)
    copies = []
    for step in range(1, slots):
        copy = remote(
            x_ref, plane_box.at[step], send.at[step], recv.at[step], plane_peer(step)
        )
        copy.start()
        copies.append(copy)
    total = x_ref[...]
    for copy in copies:
        copy.wait_recv()
    for step in range(1, slots):
        total = total + plane_box[step]
    plane_sum[...] = total
    lines = []
    for step in range(1, ctxs):
        copy = remote(
            plane_sum, line_box.at[step], line_send.at[step], line_recv.at[step], line_peer(step)
        )
        copy.start()
        lines.append(copy)
    for copy in lines:
        copy.wait_recv()
    for step in range(1, ctxs):
        total = total + line_box[step]
    o_ref[...] = total
    for copy in copies + lines:
        copy.wait_send()


def small_sum(values, number):
    count = values.size
    rows = -(-count // (8 * LANES)) * 8
    block = jnp.pad(values.reshape(-1), (0, rows * LANES - count)).reshape(rows, LANES)
    slots = lax.axis_size("dp") * lax.axis_size("tensor")
    ctxs = lax.axis_size("ctx")
    total = pl.pallas_call(
        small_sum_kernel,
        out_shape=jax.ShapeDtypeStruct(block.shape, jnp.float32),
        in_specs=[pl.BlockSpec(memory_space=pltpu.VMEM)],
        out_specs=pl.BlockSpec(memory_space=pltpu.VMEM),
        scratch_shapes=[
            pltpu.VMEM((slots,) + block.shape, jnp.float32),
            pltpu.VMEM(block.shape, jnp.float32),
            pltpu.VMEM((ctxs,) + block.shape, jnp.float32),
            pltpu.SemaphoreType.DMA((slots,)),
            pltpu.SemaphoreType.DMA((slots,)),
            pltpu.SemaphoreType.DMA((ctxs,)),
            pltpu.SemaphoreType.DMA((ctxs,)),
        ],
        compiler_params=pltpu.CompilerParams(
            collective_id=number, has_side_effects=True, vmem_limit_bytes=16 << 20
        ),
    )(block)
    return total.reshape(-1)[:count]


def rms_scale(values):
    return lax.rsqrt(jnp.mean(values * values, -1, keepdims=True) + epsilon)


def rms_back(values, upstream):
    row_scale = rms_scale(values)
    normed = values * row_scale
    return row_scale * (upstream - normed * jnp.mean(upstream * normed, -1, keepdims=True))


def low(values):
    return values.astype(jnp.bfloat16)


def wide(values):
    return values.astype(jnp.float32)


def dot_nn(left, right):
    return lax.dot_general(left, right, (((1,), (0,)), ((), ())), preferred_element_type=jnp.float32)


def dot_nt(left, right):
    return lax.dot_general(left, right, (((1,), (1,)), ((), ())), preferred_element_type=jnp.float32)


def dot_tn(left, right):
    return lax.dot_general(left, right, (((0,), (0,)), ((), ())), preferred_element_type=jnp.float32)


def shifted(block, axis, distance):
    devices = range(lax.axis_size(axis))
    route = [(i - distance, i) for i in devices if i - distance in devices]
    return lax.ppermute(block, axis, route)


def rotary_tables(positions, head_dim):
    half_dim = head_dim // 2
    freqs = jnp.exp(-math.log(1000000.0) * 2.0 * jnp.arange(half_dim, dtype=jnp.float32) / head_dim)
    angles = wide(positions)[..., None] * freqs
    return (jnp.cos(angles), jnp.sin(angles))


def rotate(values, cosine, sine):
    half_dim = values.shape[-1] // 2
    first, second = values[..., :half_dim], values[..., half_dim:]
    return jnp.concatenate([first * cosine - second * sine, second * cosine + first * sine], -1)


def column_blocks(weight, count, width):
    rows, columns = weight.shape
    weight = jnp.pad(weight, ((0, 0), (0, count * width - columns)))
    return weight.reshape(rows, count, width).transpose(1, 0, 2)


def spread_weights(blocks, number):
    mine = swap_blocks(blocks, number)
    whole = lax.all_gather(mine, "ctx", axis=0, tiled=False)
    return whole.reshape(-1, whole.shape[-1])


def collect_grads(grad):
    ctx, count = lax.axis_size("ctx"), lax.axis_size("dp")
    grad = low(grad).reshape(ctx, -1, grad.shape[-1])
    summed = lax.psum_scatter(grad, "ctx", scatter_dimension=0, tiled=False)
    return summed.reshape(count, -1, summed.shape[-1])


def finish_grads(summed):
    return wide(return_blocks(summed))


def feed_forward(normed, weights, width):
    both = dot_nn(normed, weights[:, : 2 * width])
    gate, lift = both[:, :width], both[:, width:]
    hidden = low(jax.nn.silu(gate) * lift)
    partial = dot_nt(hidden, weights[:, 2 * width :])
    return partial, (gate, lift, hidden)


def feed_backward(grad_all, normed, weights, width, saved):
    gate, lift, hidden = saved
    down_grad = low(dot_tn(grad_all, hidden))
    hidden_grad = dot_nn(grad_all, after(weights[:, 2 * width :], down_grad))
    sig = jax.nn.sigmoid(gate)
    gate_grad = low(hidden_grad * lift * sig * (1.0 + gate * (1.0 - sig)))
    lift_grad = low(hidden_grad * gate * sig)
    gate_weight_grad = low(dot_tn(normed, gate_grad))
    lift_weight_grad = low(dot_tn(normed, lift_grad))
    gate_low, lift_low = lax.optimization_barrier(
        (gate_grad, lift_grad, gate_weight_grad, lift_weight_grad)
    )[:2]
    partial = dot_nt(gate_low, weights[:, :width]) + dot_nt(
        lift_low, weights[:, width : 2 * width]
    )
    return partial, (gate_weight_grad, lift_weight_grad, down_grad)


def shards(
    hidden_in,
    doc_pos,
    mixer_gain,
    mixer_in,
    conv_taps,
    mixer_out,
    feed_first,
    gate_first,
    lift_first,
    down_first,
    attend_gain,
    query_proj,
    key_proj,
    value_proj,
    query_gain,
    key_gain,
    attend_out,
    feed_second,
    gate_second,
    lift_second,
    down_second,
    output_grad,
):
    dp, ten, ctx = (lax.axis_index(name) for name in ("dp", "tensor", "ctx"))
    seqs, tens, ctxs = (lax.axis_size(name) for name in ("dp", "tensor", "ctx"))
    rows, width = hidden_in.shape[1], hidden_in.shape[2]
    own_rows = rows // tens
    part = mixer_gain.shape[0]
    channels = mixer_in.shape[2] // seqs
    units = gate_first.shape[1]
    feed_width = -(-units // (seqs * LANES)) * LANES

    def regroup(values):
        lead = values.shape[:-1]
        return values.reshape(lead + (seqs, ctxs, part)).swapaxes(-3, -2).reshape(lead + (width,))

    def restore(values):
        lead = values.shape[:-1]
        return values.reshape(lead + (ctxs, seqs, part)).swapaxes(-3, -2).reshape(lead + (width,))

    mixer_blocks = jnp.concatenate(
        [column_blocks(mixer_in[k], seqs, channels) for k in range(3)]
        + [column_blocks(mixer_out.T, seqs, channels)],
        -1,
    )
    own_gains = jnp.stack([mixer_gain, feed_first, attend_gain, feed_second], 1)
    own_gains = jnp.pad(own_gains, ((0, 0), (0, LANES - 4)))
    own_gains = jnp.broadcast_to(own_gains, (seqs, part, LANES))
    mixer_w = spread_weights(jnp.concatenate([mixer_blocks, own_gains], -1), 3)
    gains = wide(mixer_w[:, 4 * channels : 4 * channels + 4]).T
    first_blocks = jnp.concatenate(
        [column_blocks(w, seqs, feed_width) for w in (gate_first, lift_first, down_first.T)], -1
    )
    first_w = spread_weights(first_blocks, 4)
    q_cols, kv_cols = query_proj.shape[1] // seqs, key_proj.shape[1] // seqs
    attend_blocks = jnp.concatenate(
        [
            column_blocks(query_proj, seqs, q_cols),
            column_blocks(key_proj, seqs, kv_cols),
            column_blocks(value_proj, seqs, kv_cols),
            column_blocks(attend_out.T, seqs, q_cols),
        ],
        -1,
    )
    attend_w = spread_weights(attend_blocks, 6)
    second_blocks = jnp.concatenate(
        [column_blocks(w, seqs, feed_width) for w in (gate_second, lift_second, down_second.T)], -1
    )
    second_w = spread_weights(second_blocks, 4)

    positions = from_all_dp(doc_pos)
    own_taps = wide(lax.dynamic_slice_in_dim(conv_taps, dp * channels, channels, 1))

    def own_half(values):
        return regroup(lax.dynamic_slice_in_dim(values[0], ten * own_rows, own_rows, 0))

    stream_zero = wide(own_half(hidden_in))
    upstream = wide(own_half(output_grad))

    def norm_rows(stream, gain):
        return low(stream * rms_scale(stream) * gain)

    mixer_norm = plane_gather(norm_rows(stream_zero, gains[0]))
    mixer_in_w, mixer_out_w = mixer_w[:, : 3 * channels], mixer_w[:, 3 * channels : 4 * channels]
    projected = dot_nn(mixer_norm, mixer_in_w).reshape(seqs, rows, 3 * channels)
    gate_b = projected[..., :channels]
    gate_c = projected[..., channels : 2 * channels]
    conv_input = projected[..., 2 * channels :]
    conv_src = low(gate_b * conv_input)
    earlier = shifted(conv_src[:, -2:], "ctx", 1)
    extended = wide(jnp.concatenate([earlier, conv_src], 1))
    in_doc = [wide(positions >= offset)[..., None] for offset in range(3)]
    conv_sum = sum(
        own_taps[j] * extended[:, 2 - j : 2 - j + rows] * in_doc[j] for j in range(3)
    )
    conv_gated = low(gate_c * conv_sum).reshape(seqs * rows, channels)
    stream_one = stream_zero + plane_scatter(dot_nt(conv_gated, mixer_out_w))

    first_norm = plane_gather(norm_rows(stream_one, gains[1]))
    partial, first_saved = feed_forward(first_norm, first_w, feed_width)
    stream_two = stream_one + plane_scatter(partial)

    attend_norm = plane_gather(norm_rows(stream_two, gains[2]))
    qkv_w = attend_w[:, : q_cols + 2 * kv_cols]
    attend_out_w = attend_w[:, q_cols + 2 * kv_cols :]
    qkv = dot_nn(attend_norm, qkv_w).reshape(seqs, rows, -1)
    queries = qkv[..., :q_cols].reshape(seqs, rows, -1, HD)
    keys = qkv[..., q_cols : q_cols + kv_cols].reshape(seqs, rows, -1, HD)
    values = qkv[..., q_cols + kv_cols :].reshape(seqs, rows, -1, HD)
    cosine, sine = (table[:, :, None] for table in rotary_tables(positions, HD))
    query_scale, key_scale = rms_scale(queries), rms_scale(keys)
    q_gain, k_gain = wide(query_gain), wide(key_gain)
    query_rot = low(rotate(queries * query_scale * q_gain, cosine, sine))
    key_rot = low(rotate(keys * key_scale * k_gain, cosine, sine))
    kv_own = jnp.stack([key_rot, low(values)])
    kv_all = jnp.concatenate(
        [shifted(kv_own, "ctx", distance) for distance in range(ctxs - 1, 0, -1)] + [kv_own], 2
    )
    key_all, value_all = kv_all[0], kv_all[1]
    key_rows = key_all.shape[1]
    heads = kv_cols // HD
    query_g = query_rot.reshape(seqs, rows, heads, GROUPS, HD)
    query_at = jnp.arange(rows, dtype=jnp.int32) + (key_rows - rows)
    query_from = query_at[None] - positions
    key_at = jnp.arange(key_rows, dtype=jnp.int32)
    allowed = (key_at <= query_at[None, :, None]) & (key_at >= query_from[..., None])
    allowed = allowed[:, None, None]
    root = 1.0 / math.sqrt(HD)
    scores = (
        jnp.einsum("sthgd,suhd->shgtu", query_g, key_all, preferred_element_type=jnp.float32) * root
    )
    scores = jnp.where(allowed, scores, -1e30)
    top = jnp.max(scores, -1, keepdims=True)
    weights = jnp.exp(scores - top)
    probs = weights / jnp.sum(weights, -1, keepdims=True)
    probs_low = low(probs)
    context = low(
        jnp.einsum("shgtu,suhd->sthgd", probs_low, value_all, preferred_element_type=jnp.float32)
    ).reshape(seqs * rows, q_cols)
    stream_three = stream_two + plane_scatter(dot_nt(context, attend_out_w))

    second_norm = plane_gather(norm_rows(stream_three, gains[3]))
    partial, second_saved = feed_forward(second_norm, second_w, feed_width)
    stream_four = stream_three + plane_scatter(partial)

    def both_halves(values):
        values = low(restore(values))
        other = lax.ppermute(values, "tensor", [(i, 1 - i) for i in range(tens)])
        lower = lax.select_n(ten, values, other)
        upper = lax.select_n(ten, other, values)
        return jnp.concatenate([lower, upper], 0)[None]

    hidden_out = both_halves(stream_four)

    def norm_step(upstream, stream, gain, normed_grad):
        gain_grad = jnp.sum(normed_grad * stream * rms_scale(stream), 0)
        return upstream + rms_back(stream, normed_grad * gain), gain_grad

    grad_all = plane_gather(low(upstream))
    partial, second_grads = feed_backward(grad_all, second_norm, second_w, feed_width, second_saved)
    second_sums = [collect_grads(g) for g in second_grads]
    grad_three, second_gain_grad = norm_step(
        upstream, stream_three, gains[3], plane_scatter(partial)
    )
    grad_three = after(grad_three, second_sums[2])

    grad_all = plane_gather(low(grad_three))
    attend_out_grad = dot_tn(grad_all, context)
    context_grad = low(dot_nn(grad_all, attend_out_w)).reshape(seqs, rows, heads, GROUPS, HD)
    prob_grad = jnp.einsum(
        "sthgd,suhd->shgtu", context_grad, value_all, preferred_element_type=jnp.float32
    )
    delta = jnp.sum(probs * prob_grad, -1, keepdims=True)
    score_grad = low(probs * (prob_grad - delta))
    query_acc = (
        jnp.einsum("shgtu,suhd->sthgd", score_grad, key_all, preferred_element_type=jnp.float32)
        * root
    ).reshape(seqs, rows, -1, HD)
    key_acc = (
        jnp.einsum("shgtu,sthgd->suhd", score_grad, query_g, preferred_element_type=jnp.float32)
        * root
    )
    value_acc = jnp.einsum(
        "shgtu,sthgd->suhd", probs_low, context_grad, preferred_element_type=jnp.float32
    )
    kv_acc = low(jnp.stack([key_acc, value_acc])).reshape(2, seqs, ctxs, rows, heads, HD)
    kv_mine = wide(kv_acc[:, :, ctxs - 1])
    for distance in range(1, ctxs):
        kv_mine = kv_mine + wide(shifted(kv_acc[:, :, ctxs - 1 - distance], "ctx", -distance))
    query_norm_grad = rotate(query_acc, cosine, -sine)
    key_norm_grad = rotate(kv_mine[0], cosine, -sine)
    query_gain_part = jnp.sum(query_norm_grad * queries * query_scale, (0, 1, 2))
    key_gain_part = jnp.sum(key_norm_grad * keys * key_scale, (0, 1, 2))
    query_grad = low(rms_back(queries, query_norm_grad * q_gain)).reshape(seqs * rows, -1)
    key_grad = low(rms_back(keys, key_norm_grad * k_gain)).reshape(seqs * rows, -1)
    value_grad = low(kv_mine[1]).reshape(seqs * rows, -1)
    qkv_grad = jnp.concatenate([query_grad, key_grad, value_grad], -1)
    qkv_weight_grad = dot_tn(attend_norm, qkv_grad)
    attend_grads = low(jnp.concatenate([qkv_weight_grad, attend_out_grad], -1))
    attend_sums = collect_grads(attend_grads)
    grad_two, attend_gain_grad = norm_step(
        grad_three,
        stream_two,
        gains[2],
        plane_scatter(after(low(dot_nt(qkv_grad, qkv_w)), attend_grads)),
    )
    grad_two = after(grad_two, second_sums[0], second_sums[1])

    grad_all = plane_gather(low(grad_two))
    partial, first_grads = feed_backward(grad_all, first_norm, first_w, feed_width, first_saved)
    first_sums = [collect_grads(g) for g in first_grads]
    grad_one, first_gain_grad = norm_step(grad_two, stream_one, gains[1], plane_scatter(partial))
    grad_one = after(grad_one, attend_sums)
    second_done, first_done = (
        [finish_grads(total).reshape(part, -1)[:, :units] for total in sums]
        for sums in (second_sums, first_sums)
    )
    attend_done = finish_grads(attend_sums)

    grad_all = plane_gather(low(grad_one))
    mixer_out_grad = dot_tn(grad_all, conv_gated)
    gated_grad = dot_nn(grad_all, mixer_out_w).reshape(seqs, rows, channels)
    gate_c_grad = low(gated_grad * conv_sum)
    sum_grad = gated_grad * gate_c
    tap_rows = []
    spread = jnp.zeros_like(extended)
    for j in range(3):
        masked = sum_grad * in_doc[j]
        tap_rows.append(jnp.sum(masked * extended[:, 2 - j : 2 - j + rows], (0, 1)))
        spread = spread + jnp.pad(own_taps[j] * masked, ((0, 0), (2 - j, j), (0, 0)))
    returned = shifted(spread[:, :2], "ctx", -1)
    src_grad = spread[:, 2:] + jnp.pad(returned, ((0, 0), (rows - 2, 0), (0, 0)))
    proj_grad = jnp.concatenate(
        [low(src_grad * conv_input), gate_c_grad, low(src_grad * gate_b)], -1
    ).reshape(seqs * rows, 3 * channels)
    mixer_in_grad = dot_tn(mixer_norm, proj_grad)
    mixer_grads = low(jnp.concatenate([mixer_in_grad, mixer_out_grad], -1))
    mixer_done = finish_grads(collect_grads(mixer_grads))
    grad_zero, mixer_gain_grad = norm_step(
        grad_one,
        stream_zero,
        gains[0],
        plane_scatter(after(low(dot_nt(proj_grad, mixer_in_w)), mixer_grads)),
    )
    hidden_grad = both_halves(grad_zero)

    gain_rows = restore(
        jnp.stack([mixer_gain_grad, first_gain_grad, attend_gain_grad, second_gain_grad])
    )
    taps_part = lax.dynamic_update_slice(
        jnp.zeros((tens, 3, channels * seqs), jnp.float32),
        jnp.stack(tap_rows)[None],
        (ten, 0, dp * channels),
    )
    small = jnp.concatenate(
        [gain_rows.reshape(-1), query_gain_part, key_gain_part, taps_part.reshape(-1)]
    )
    small = small_sum(small, 5)
    gain_sums = lax.dynamic_slice_in_dim(
        small[: 4 * width].reshape(4, width), (dp * ctxs + ctx) * part, part, 1
    )
    query_gain_grad = small[4 * width : 4 * width + HD]
    key_gain_grad = small[4 * width + HD : 4 * width + 2 * HD]
    taps_grad = lax.dynamic_index_in_dim(
        small[4 * width + 2 * HD :].reshape(tens, 3, channels * seqs), ten, 0, keepdims=False
    )

    def columns(done, start, count):
        return done[:, :, start : start + count].reshape(part, -1)

    return (
        hidden_out,
        hidden_grad,
        gain_sums[0],
        jnp.stack([columns(mixer_done, k * channels, channels) for k in range(3)]),
        taps_grad,
        columns(mixer_done, 3 * channels, channels).T,
        gain_sums[1],
        first_done[0],
        first_done[1],
        first_done[2].T,
        gain_sums[2],
        columns(attend_done, 0, q_cols),
        columns(attend_done, q_cols, kv_cols),
        columns(attend_done, q_cols + kv_cols, kv_cols),
        query_gain_grad,
        key_gain_grad,
        columns(attend_done, q_cols + 2 * kv_cols, q_cols).T,
        gain_sums[3],
        second_done[0],
        second_done[1],
        second_done[2].T,
    )


def solution(mesh):
    rows = P("dp", "ctx", None)
    gain = P(("dp", "ctx"))
    into = P(("dp", "ctx"), "tensor")
    out = P("tensor", ("dp", "ctx"))
    thrice = P(None, ("dp", "ctx"), "tensor")
    taps = P(None, "tensor")
    weights = (
        (gain, thrice, taps, out, gain, into, into, out)
        + (gain, into, into, into, P(), P(), out)
        + (gain, into, into, out)
    )
    return jax.shard_map(
        shards,
        mesh=mesh,
        in_specs=(rows, P("dp", "ctx")) + weights + (rows,),
        out_specs=(rows, rows) + weights,
        check_vma=False,
    )
```

```python
import functools
import math

import jax
import jax.numpy as jnp
from jax import lax
from jax.experimental import pallas as pl
from jax.experimental.pallas import tpu as pltpu
from jax.sharding import PartitionSpec as P

H = 24
KV = 8
HD = 64
GROUPS = H // KV
LANES = 128

epsilon = 1e-05
MESH = pl.DeviceIdType.MESH


def plane_place():
    dp = lax.axis_index("dp")
    ten = lax.axis_index("tensor")
    core = lax.rem(dp, 2)
    across = lax.rem(dp + 2, 4)
    twin = dp + 1 - 2 * core
    return dp, ten, core, across, twin


def greet(dp, ten, across, twin):
    barrier = pltpu.get_barrier_semaphore()
    pl.semaphore_signal(barrier, 1, device_id={"dp": across}, device_id_type=MESH)
    pl.semaphore_signal(barrier, 1, device_id={"tensor": 1 - ten}, device_id_type=MESH)
    pl.semaphore_signal(barrier, 1, device_id={"dp": twin}, device_id_type=MESH)
    pl.semaphore_wait(barrier, 3)


def remote(src, dst, send, recv, place):
    return pltpu.make_async_remote_copy(
        src_ref=src,
        dst_ref=dst,
        send_sem=send,
        recv_sem=recv,
        device_id=place,
        device_id_type=MESH,
    )


def gather_kernel(x_ref, o_ref, own_sem, send, recv):
    dp, ten, core, across, twin = plane_place()
    greet(dp, ten, across, twin)
    to_across = {"dp": across, "tensor": ten}
    to_side = {"dp": dp, "tensor": 1 - ten}
    to_twin = {"dp": twin, "tensor": ten}
    own = dp * 2 + ten
    first = (across * (1 - core) + dp * core) * 2 + ten * (1 - core) + (1 - ten) * core
    other = (dp * (1 - core) + across * core) * 2 + (1 - ten) * (1 - core) + ten * core
    onward = {
        "dp": dp * (1 - core) + across * core,
        "tensor": (1 - ten) * (1 - core) + ten * core,
    }
    far = across * 2 + 1 - ten

    def move(src, slot, number, place):
        copy = remote(src, o_ref.at[slot], send.at[number], recv.at[slot], place)
        copy.start()
        return copy

    copies = [
        move(x_ref, own, 0, to_across),
        move(x_ref, own, 1, to_side),
        move(x_ref, own, 2, to_twin),
    ]
    local = pltpu.make_async_copy(x_ref, o_ref.at[own], own_sem)
    local.start()

    def arrived(slot):
        remote(x_ref, o_ref.at[slot], send.at[0], recv.at[slot], to_twin).wait_recv()

    arrived(first)
    copies.append(move(o_ref.at[first], first, 3, onward))
    copies.append(move(o_ref.at[first], first, 4, to_twin))
    arrived(other)
    copies.append(move(o_ref.at[other], other, 5, to_twin))
    arrived(far)
    copies.append(move(o_ref.at[far], far, 6, to_twin))
    twin_across = lax.rem(twin + 2, 4)
    for there in (twin, twin_across):
        for side in range(2):
            arrived(there * 2 + side)
    local.wait()
    for copy in copies:
        copy.wait_send()


def plane_gather(block):
    rows, width = block.shape
    slots = lax.axis_size("dp") * lax.axis_size("tensor")
    gathered = pl.pallas_call(
        gather_kernel,
        out_shape=jax.ShapeDtypeStruct((slots, rows, width), block.dtype),
        in_specs=[pl.BlockSpec(memory_space=pltpu.VMEM)],
        out_specs=pl.BlockSpec(memory_space=pl.ANY),
        scratch_shapes=[
            pltpu.SemaphoreType.DMA,
            pltpu.SemaphoreType.DMA((7,)),
            pltpu.SemaphoreType.DMA((8,)),
        ],
        compiler_params=pltpu.CompilerParams(
            collective_id=1, has_side_effects=True, vmem_limit_bytes=16 << 20
        ),
    )(block)
    return gathered.reshape(slots * rows, width)


def scatter_kernel(p_ref, o_ref, mine, theirs, out_box, in_box, load, send, recv):
    dp, ten, core, across, twin = plane_place()
    greet(dp, ten, across, twin)
    twin_across = lax.rem(twin + 2, 4)
    to_twin = {"dp": twin, "tensor": ten}
    sides = (ten, 1 - ten, ten, 1 - ten)
    home = (dp, dp, across, across)
    away = (twin, twin, twin_across, twin_across)
    order = (3, 1, 2, 0)
    loads = {}
    gifts = {}
    for rel in order:
        gifts[rel] = remote(
            p_ref.at[away[rel] * 2 + sides[rel]],
            theirs.at[rel],
            send.at[rel],
            recv.at[rel],
            to_twin,
        )
        gifts[rel].start()
        loads[rel] = pltpu.make_async_copy(
            p_ref.at[home[rel] * 2 + sides[rel]], mine.at[rel], load.at[rel]
        )
        loads[rel].start()
    direct = 1 + core
    relayed = 2 - core
    to_direct = {
        "dp": dp * (1 - core) + across * core,
        "tensor": (1 - ten) * (1 - core) + ten * core,
    }
    to_relayed = {
        "dp": across * (1 - core) + dp * core,
        "tensor": ten * (1 - core) + (1 - ten) * core,
    }

    def total(rel):
        return mine[rel].astype(jnp.float32) + theirs[rel].astype(jnp.float32)

    def post(number, value, place):
        out_box[number] = value.astype(out_box.dtype)
        copy = remote(
            out_box.at[number], in_box.at[number], send.at[4 + number], recv.at[4 + number], place
        )
        copy.start()
        return copy

    loads[3].wait()
    gifts[3].wait_recv()
    relay = post(0, total(3), to_direct)
    for rel in (1, 2):
        loads[rel].wait()
        gifts[rel].wait_recv()
    straight = post(1, total(direct), to_direct)
    relay.wait_recv()
    bent = post(2, total(relayed) + in_box[0].astype(jnp.float32), to_relayed)
    loads[0].wait()
    gifts[0].wait_recv()
    partial = total(0)
    straight.wait_recv()
    partial = partial + in_box[1].astype(jnp.float32)
    bent.wait_recv()
    o_ref[...] = partial + in_box[2].astype(jnp.float32)
    for rel in order:
        gifts[rel].wait_send()
    for copy in (relay, straight, bent):
        copy.wait_send()


def plane_scatter(partial):
    slots = lax.axis_size("dp") * lax.axis_size("tensor")
    rows, width = partial.shape[0] // slots, partial.shape[1]
    block = (rows, width)
    return pl.pallas_call(
        scatter_kernel,
        out_shape=jax.ShapeDtypeStruct(block, jnp.float32),
        in_specs=[pl.BlockSpec(memory_space=pl.ANY)],
        out_specs=pl.BlockSpec(memory_space=pltpu.VMEM),
        scratch_shapes=[
            pltpu.VMEM((4,) + block, jnp.bfloat16),
            pltpu.VMEM((4,) + block, jnp.bfloat16),
            pltpu.VMEM((3,) + block, jnp.bfloat16),
            pltpu.VMEM((3,) + block, jnp.bfloat16),
            pltpu.SemaphoreType.DMA((4,)),
            pltpu.SemaphoreType.DMA((7,)),
            pltpu.SemaphoreType.DMA((7,)),
        ],
        compiler_params=pltpu.CompilerParams(
            collective_id=2, has_side_effects=True, vmem_limit_bytes=24 << 20
        ),
    )(partial.astype(jnp.bfloat16).reshape((slots,) + block))


def swap_kernel(x_ref, o_ref, own_sem, send, recv):
    dp = lax.axis_index("dp")
    ten = lax.axis_index("tensor")
    barrier = pltpu.get_barrier_semaphore()
    for step in (1, 2, 3):
        pl.semaphore_signal(
            barrier,
            1,
            device_id={"dp": lax.rem(dp + step, 4), "tensor": ten},
            device_id_type=MESH,
        )
    pl.semaphore_wait(barrier, 3)
    copies = []
    for step in (2, 1, 3):
        there = lax.rem(dp + step, 4)
        copy = remote(
            x_ref.at[there],
            o_ref.at[dp],
            send.at[step],
            recv.at[step],
            {"dp": there, "tensor": ten},
        )
        copy.start()
        copies.append(copy)
    local = pltpu.make_async_copy(x_ref.at[dp], o_ref.at[dp], own_sem)
    local.start()
    for copy in copies:
        copy.wait()
    local.wait()


def turn_kernel(x_ref, o_ref, own_sem, send, recv):
    dp = lax.axis_index("dp")
    ten = lax.axis_index("tensor")
    barrier = pltpu.get_barrier_semaphore()
    for step in (1, 2, 3):
        pl.semaphore_signal(
            barrier,
            1,
            device_id={"dp": lax.rem(dp + step, 4), "tensor": ten},
            device_id_type=MESH,
        )
    pl.semaphore_wait(barrier, 3)
    copies = []
    for step in (2, 1, 3):
        there = lax.rem(dp + step, 4)
        copy = remote(
            x_ref.at[there],
            o_ref.at[:, dp],
            send.at[step],
            recv.at[step],
            {"dp": there, "tensor": ten},
        )
        copy.start()
        copies.append(copy)
    local = pltpu.make_async_copy(x_ref.at[dp], o_ref.at[:, dp], own_sem)
    local.start()
    for copy in copies:
        copy.wait()
    local.wait()


def turn_blocks(blocks, number):
    shape = (blocks.shape[1], blocks.shape[0]) + blocks.shape[2:]
    return pl.pallas_call(
        turn_kernel,
        out_shape=jax.ShapeDtypeStruct(shape, blocks.dtype),
        in_specs=[pl.BlockSpec(memory_space=pltpu.VMEM)],
        out_specs=pl.BlockSpec(memory_space=pl.ANY),
        scratch_shapes=[
            pltpu.SemaphoreType.DMA,
            pltpu.SemaphoreType.DMA((4,)),
            pltpu.SemaphoreType.DMA((4,)),
        ],
        compiler_params=pltpu.CompilerParams(
            collective_id=number, has_side_effects=True, vmem_limit_bytes=16 << 20
        ),
    )(blocks)


def swap_blocks(blocks, number):
    return pl.pallas_call(
        swap_kernel,
        out_shape=jax.ShapeDtypeStruct(blocks.shape, blocks.dtype),
        in_specs=[pl.BlockSpec(memory_space=pltpu.VMEM)],
        out_specs=pl.BlockSpec(memory_space=pl.ANY),
        scratch_shapes=[
            pltpu.SemaphoreType.DMA,
            pltpu.SemaphoreType.DMA((4,)),
            pltpu.SemaphoreType.DMA((4,)),
        ],
        compiler_params=pltpu.CompilerParams(
            collective_id=number, has_side_effects=True, vmem_limit_bytes=16 << 20
        ),
    )(blocks)


def send_back(blocks):
    dp = lax.axis_index("dp")
    devices = range(lax.axis_size("dp"))
    parts = [lax.dynamic_index_in_dim(blocks, dp, 0, keepdims=False)]
    for flip in (1, 2, 3):
        sent = lax.dynamic_index_in_dim(blocks, dp ^ flip, 0, keepdims=False)
        parts.append(lax.ppermute(sent, "dp", [(i, i ^ flip) for i in devices]))
    return parts


def by_source(parts):
    dp = lax.axis_index("dp")
    devices = range(lax.axis_size("dp"))
    return jnp.stack([wide(lax.select_n(dp, *(parts[j ^ i] for i in devices))) for j in devices], 1)


def from_all_dp(block):
    dp = lax.axis_index("dp")
    devices = range(lax.axis_size("dp"))
    parts = [block] + [
        lax.ppermute(block, "dp", [(i, i ^ flip) for i in devices]) for flip in (1, 2, 3)
    ]
    return jnp.concatenate([lax.select_n(dp, *(parts[j ^ i] for i in devices)) for j in devices], 0)


def together(*values):
    return lax.optimization_barrier(values)


def small_sum_kernel(x_ref, o_ref, plane_box, plane_sum, line_box, send, recv, line_send, line_recv):
    dp, ten, ctx = (lax.axis_index(name) for name in ("dp", "tensor", "ctx"))
    dps, tens, ctxs = (lax.axis_size(name) for name in ("dp", "tensor", "ctx"))
    slots = dps * tens
    own = dp * tens + ten
    barrier = pltpu.get_barrier_semaphore()

    def plane_peer(step):
        slot = lax.rem(own + step, slots)
        return {"dp": slot // tens, "tensor": lax.rem(slot, tens), "ctx": ctx}

    def line_peer(step):
        return {"dp": dp, "tensor": ten, "ctx": lax.rem(ctx + step, ctxs)}

    for step in range(1, slots):
        pl.semaphore_signal(barrier, 1, device_id=plane_peer(step), device_id_type=MESH)
    for step in range(1, ctxs):
        pl.semaphore_signal(barrier, 1, device_id=line_peer(step), device_id_type=MESH)
    pl.semaphore_wait(barrier, slots + ctxs - 2)
    copies = []
    for step in range(1, slots):
        copy = remote(
            x_ref, plane_box.at[step], send.at[step], recv.at[step], plane_peer(step)
        )
        copy.start()
        copies.append(copy)
    total = x_ref[...]
    for copy in copies:
        copy.wait_recv()
    for step in range(1, slots):
        total = total + plane_box[step]
    plane_sum[...] = total
    lines = []
    for step in range(1, ctxs):
        copy = remote(
            plane_sum, line_box.at[step], line_send.at[step], line_recv.at[step], line_peer(step)
        )
        copy.start()
        lines.append(copy)
    for copy in lines:
        copy.wait_recv()
    for step in range(1, ctxs):
        total = total + line_box[step]
    o_ref[...] = total
    for copy in copies + lines:
        copy.wait_send()


def small_gather_kernel(x_ref, o_ref, own_sem, send, recv, line_send, line_recv):
    dp, ten, ctx = (lax.axis_index(name) for name in ("dp", "tensor", "ctx"))
    dps, ctxs = (lax.axis_size(name) for name in ("dp", "ctx"))
    barrier = pltpu.get_barrier_semaphore()

    def dp_peer(step):
        return {"dp": lax.rem(dp + step, dps), "tensor": ten, "ctx": ctx}

    def ctx_peer(step):
        return {"dp": dp, "tensor": ten, "ctx": lax.rem(ctx + step, ctxs)}

    for step in range(1, dps):
        pl.semaphore_signal(barrier, 1, device_id=dp_peer(step), device_id_type=MESH)
    for step in range(1, ctxs):
        pl.semaphore_signal(barrier, 1, device_id=ctx_peer(step), device_id_type=MESH)
    pl.semaphore_wait(barrier, dps + ctxs - 2)
    copies = []
    for step in range(1, dps):
        copy = remote(x_ref, o_ref.at[ctx, dp], send.at[step], recv.at[step], dp_peer(step))
        copy.start()
        copies.append(copy)
    local = pltpu.make_async_copy(x_ref, o_ref.at[ctx, dp], own_sem)
    local.start()
    local.wait()
    for copy in copies:
        copy.wait()
    lines = []
    for step in range(1, ctxs):
        copy = remote(
            o_ref.at[ctx], o_ref.at[ctx], line_send.at[step], line_recv.at[step], ctx_peer(step)
        )
        copy.start()
        lines.append(copy)
    for copy in lines:
        copy.wait()


def small_gather(block, number):
    dps, ctxs = lax.axis_size("dp"), lax.axis_size("ctx")
    return pl.pallas_call(
        small_gather_kernel,
        out_shape=jax.ShapeDtypeStruct((ctxs, dps) + block.shape, block.dtype),
        in_specs=[pl.BlockSpec(memory_space=pltpu.VMEM)],
        out_specs=pl.BlockSpec(memory_space=pltpu.VMEM),
        scratch_shapes=[
            pltpu.SemaphoreType.DMA,
            pltpu.SemaphoreType.DMA((dps,)),
            pltpu.SemaphoreType.DMA((dps,)),
            pltpu.SemaphoreType.DMA((ctxs,)),
            pltpu.SemaphoreType.DMA((ctxs,)),
        ],
        compiler_params=pltpu.CompilerParams(
            collective_id=number, has_side_effects=True, vmem_limit_bytes=16 << 20
        ),
    )(block)


def small_sum(values, number):
    count = values.size
    rows = -(-count // (8 * LANES)) * 8
    block = jnp.pad(values.reshape(-1), (0, rows * LANES - count)).reshape(rows, LANES)
    slots = lax.axis_size("dp") * lax.axis_size("tensor")
    ctxs = lax.axis_size("ctx")
    total = pl.pallas_call(
        small_sum_kernel,
        out_shape=jax.ShapeDtypeStruct(block.shape, jnp.float32),
        in_specs=[pl.BlockSpec(memory_space=pltpu.VMEM)],
        out_specs=pl.BlockSpec(memory_space=pltpu.VMEM),
        scratch_shapes=[
            pltpu.VMEM((slots,) + block.shape, jnp.float32),
            pltpu.VMEM(block.shape, jnp.float32),
            pltpu.VMEM((ctxs,) + block.shape, jnp.float32),
            pltpu.SemaphoreType.DMA((slots,)),
            pltpu.SemaphoreType.DMA((slots,)),
            pltpu.SemaphoreType.DMA((ctxs,)),
            pltpu.SemaphoreType.DMA((ctxs,)),
        ],
        compiler_params=pltpu.CompilerParams(
            collective_id=number, has_side_effects=True, vmem_limit_bytes=16 << 20
        ),
    )(block)
    return total.reshape(-1)[:count]


def rms_scale(values):
    return lax.rsqrt(jnp.mean(values * values, -1, keepdims=True) + epsilon)


def rms_back(values, upstream):
    row_scale = rms_scale(values)
    normed = values * row_scale
    return row_scale * (upstream - normed * jnp.mean(upstream * normed, -1, keepdims=True))


def low(values):
    return values.astype(jnp.bfloat16)


def wide(values):
    return values.astype(jnp.float32)


def dot_nn(left, right):
    return lax.dot_general(left, right, (((1,), (0,)), ((), ())), preferred_element_type=jnp.float32)


def dot_nt(left, right):
    return lax.dot_general(left, right, (((1,), (1,)), ((), ())), preferred_element_type=jnp.float32)


def dot_tn(left, right):
    return lax.dot_general(left, right, (((0,), (0,)), ((), ())), preferred_element_type=jnp.float32)


def shifted(block, axis, distance):
    devices = range(lax.axis_size(axis))
    route = [(i - distance, i) for i in devices if i - distance in devices]
    return lax.ppermute(block, axis, route)


def rotary_tables(positions, head_dim):
    half_dim = head_dim // 2
    freqs = jnp.exp(-math.log(1000000.0) * 2.0 * jnp.arange(half_dim, dtype=jnp.float32) / head_dim)
    angles = wide(positions)[..., None] * freqs
    return (jnp.cos(angles), jnp.sin(angles))


def rotate(values, cosine, sine):
    half_dim = values.shape[-1] // 2
    first, second = values[..., :half_dim], values[..., half_dim:]
    return jnp.concatenate([first * cosine - second * sine, second * cosine + first * sine], -1)


def visible(pos_ref, rows, key_rows):
    query_at = lax.broadcasted_iota(jnp.int32, (rows, key_rows), 0) + (key_rows - rows)
    key_at = lax.broadcasted_iota(jnp.int32, (rows, key_rows), 1)
    return (key_at <= query_at) & (key_at >= query_at - pos_ref[0])


def attend_kernel(q_ref, kv_ref, pos_ref, context_ref, lse_ref):
    rows = q_ref.shape[1]
    key_rows = kv_ref.shape[0] * rows
    both = kv_ref[...].reshape(key_rows, 2 * HD)
    keys, values = both[:, :HD], both[:, HD:]
    allowed = visible(pos_ref, rows, key_rows)
    contexts, totals = [], []
    for head in range(GROUPS):
        query = q_ref[0, :, head * HD : (head + 1) * HD]
        scores = jnp.where(allowed, dot_nt(query, keys) * (1.0 / math.sqrt(HD)), -1e30)
        top = jnp.max(scores, -1, keepdims=True)
        weights = jnp.exp(scores - top)
        total = jnp.sum(weights, -1, keepdims=True)
        contexts.append(low(dot_nn(low(weights * (1.0 / total)), values)))
        totals.append(top + jnp.log(total))
    context_ref[0] = jnp.concatenate(contexts, -1)
    lse_ref[0] = jnp.concatenate(totals + [jnp.zeros_like(totals[0])] * (8 - GROUPS), -1)


def attend_back_kernel(q_ref, kv_ref, pos_ref, lse_ref, grad_ref, dq_ref, dkv_ref):
    rows = q_ref.shape[1]
    key_rows = kv_ref.shape[0] * rows
    both = kv_ref[...].reshape(key_rows, 2 * HD)
    keys, values = both[:, :HD], both[:, HD:]
    allowed = visible(pos_ref, rows, key_rows)
    root = 1.0 / math.sqrt(HD)
    query_grads = []
    key_grad = jnp.zeros((key_rows, HD), jnp.float32)
    value_grad = jnp.zeros((key_rows, HD), jnp.float32)
    for head in range(GROUPS):
        query = q_ref[0, :, head * HD : (head + 1) * HD]
        grad = grad_ref[0, :, head * HD : (head + 1) * HD]
        scores = dot_nt(query, keys) * root - lse_ref[0, :, head : head + 1]
        probs = jnp.where(allowed, jnp.exp(jnp.where(allowed, scores, 0.0)), 0.0)
        prob_grad = dot_nt(grad, values)
        delta = jnp.sum(probs * prob_grad, -1, keepdims=True)
        score_grad = low(probs * (prob_grad - delta))
        query_grads.append(dot_nn(score_grad, keys) * root)
        key_grad = key_grad + dot_tn(score_grad, query)
        value_grad = value_grad + dot_tn(low(probs), grad)
    dq_ref[0] = jnp.concatenate(query_grads, -1)
    whole = low(jnp.concatenate([key_grad * root, value_grad], -1))
    dkv_ref[...] = whole.reshape(dkv_ref.shape)


def attend_specs(seqs, rows, parts):
    by_seq = lambda width: pl.BlockSpec((1, rows, width), lambda s: (s, 0, 0))
    over_keys = pl.BlockSpec((parts, 1, rows, 2 * HD), lambda s: (0, s, 0, 0))
    return by_seq, over_keys


def attend(queries, kv_all, positions):
    seqs, rows, width = queries.shape
    by_seq, over_keys = attend_specs(seqs, rows, kv_all.shape[0])
    return pl.pallas_call(
        attend_kernel,
        grid=(seqs,),
        out_shape=(
            jax.ShapeDtypeStruct(queries.shape, jnp.bfloat16),
            jax.ShapeDtypeStruct((seqs, rows, 8), jnp.float32),
        ),
        in_specs=[by_seq(width), over_keys, by_seq(1)],
        out_specs=(by_seq(width), by_seq(8)),
        compiler_params=pltpu.CompilerParams(vmem_limit_bytes=56 << 20),
    )(queries, kv_all, positions[..., None])


def attend_back(queries, kv_all, positions, totals, grads):
    seqs, rows, width = queries.shape
    by_seq, over_keys = attend_specs(seqs, rows, kv_all.shape[0])
    return pl.pallas_call(
        attend_back_kernel,
        grid=(seqs,),
        out_shape=(
            jax.ShapeDtypeStruct(queries.shape, jnp.float32),
            jax.ShapeDtypeStruct(kv_all.shape, jnp.bfloat16),
        ),
        in_specs=[by_seq(width), over_keys, by_seq(1), by_seq(8), by_seq(width)],
        out_specs=(by_seq(width), over_keys),
        compiler_params=pltpu.CompilerParams(vmem_limit_bytes=56 << 20),
    )(queries, kv_all, positions[..., None], totals, grads)


def column_blocks(weight, count, width):
    rows, columns = weight.shape
    weight = jnp.pad(weight, ((0, 0), (0, count * width - columns)))
    return weight.reshape(rows, count, width).transpose(1, 0, 2)


def spread_weights(blocks, number):
    mine = swap_blocks(blocks, number)
    whole = lax.all_gather(mine, "ctx", axis=0, tiled=False)
    return whole.reshape(-1, whole.shape[-1])


def collect_grads(grad):
    ctx, count = lax.axis_size("ctx"), lax.axis_size("dp")
    grad = low(grad).reshape(ctx, -1, grad.shape[-1])
    summed = lax.psum_scatter(grad, "ctx", scatter_dimension=0, tiled=False)
    return summed.reshape(count, -1, summed.shape[-1])


def feed_hidden(normed, weights, width):
    both = dot_nn(normed, weights[:, : 2 * width])
    gate, lift = both[:, :width], both[:, width:]
    return gate, lift, low(jax.nn.silu(gate) * lift)


def feed_down(hidden, weights, width):
    return low(dot_nt(hidden, weights[:, 2 * width :]))


def feed_backward(grad_all, normed, weights, width, saved):
    gate, lift, hidden = saved
    down_grad, grad_all = together(low(dot_tn(grad_all, hidden)), grad_all)
    hidden_grad = dot_nn(grad_all, weights[:, 2 * width :])
    sig = jax.nn.sigmoid(gate)
    gate_grad = low(hidden_grad * lift * sig * (1.0 + gate * (1.0 - sig)))
    lift_grad = low(hidden_grad * gate * sig)
    gate_weight_grad = low(dot_tn(normed, gate_grad))
    lift_weight_grad = low(dot_tn(normed, lift_grad))
    gate_grad, lift_grad, gate_weight_grad, lift_weight_grad = together(
        gate_grad, lift_grad, gate_weight_grad, lift_weight_grad
    )
    partial = dot_nt(gate_grad, weights[:, :width]) + dot_nt(
        lift_grad, weights[:, width : 2 * width]
    )
    return partial, (gate_weight_grad, lift_weight_grad, down_grad)


def shards(
    hidden_in,
    doc_pos,
    mixer_gain,
    mixer_in,
    conv_taps,
    mixer_out,
    feed_first,
    gate_first,
    lift_first,
    down_first,
    attend_gain,
    query_proj,
    key_proj,
    value_proj,
    query_gain,
    key_gain,
    attend_out,
    feed_second,
    gate_second,
    lift_second,
    down_second,
    output_grad,
):
    dp, ten, ctx = (lax.axis_index(name) for name in ("dp", "tensor", "ctx"))
    seqs, tens, ctxs = (lax.axis_size(name) for name in ("dp", "tensor", "ctx"))
    rows, width = hidden_in.shape[1], hidden_in.shape[2]
    own_rows = rows // tens
    part = mixer_gain.shape[0]
    channels = mixer_in.shape[2] // seqs
    units = gate_first.shape[1]
    feed_width = -(-units // (seqs * LANES)) * LANES

    def regroup(values):
        lead = values.shape[:-1]
        return values.reshape(lead + (seqs, ctxs, part)).swapaxes(-3, -2).reshape(lead + (width,))

    def restore(values):
        lead = values.shape[:-1]
        return values.reshape(lead + (ctxs, seqs, part)).swapaxes(-3, -2).reshape(lead + (width,))

    def own_half(values):
        return regroup(lax.dynamic_slice_in_dim(values[0], ten * own_rows, own_rows, 0))

    stream_zero = wide(own_half(hidden_in))
    upstream = wide(own_half(output_grad))
    last_grad_all = plane_gather(low(upstream))

    def norm_rows(stream, gain):
        return low(stream * rms_scale(stream) * gain)

    mixer_blocks = jnp.concatenate(
        [column_blocks(mixer_in[k], seqs, channels) for k in range(3)]
        + [column_blocks(mixer_out.T, seqs, channels)],
        -1,
    )
    mixer_w = spread_weights(mixer_blocks, 3)
    own_gains = wide(jnp.stack([mixer_gain, feed_first, attend_gain, feed_second]))
    own_gains = jnp.pad(own_gains, ((0, 4), (0, -part % LANES)))
    gains = small_gather(own_gains, 8)[:, :, :4, :part]
    gains = gains.transpose(2, 0, 1, 3).reshape(4, width)
    first_blocks = jnp.concatenate(
        [column_blocks(w, seqs, feed_width) for w in (gate_first, lift_first, down_first.T)], -1
    )
    first_w = spread_weights(first_blocks, 4)
    q_cols, kv_cols = query_proj.shape[1] // seqs, key_proj.shape[1] // seqs
    attend_blocks = jnp.concatenate(
        [
            column_blocks(query_proj, seqs, q_cols),
            column_blocks(key_proj, seqs, kv_cols),
            column_blocks(value_proj, seqs, kv_cols),
            column_blocks(attend_out.T, seqs, q_cols),
        ],
        -1,
    )
    attend_w = spread_weights(attend_blocks, 6)
    second_blocks = jnp.concatenate(
        [column_blocks(w, seqs, feed_width) for w in (gate_second, lift_second, down_second.T)], -1
    )
    second_w = spread_weights(second_blocks, 4)

    positions = from_all_dp(doc_pos)
    mixer_norm = plane_gather(norm_rows(stream_zero, gains[0]))
    mixer_w, mixer_norm, last_grad_all = together(mixer_w, mixer_norm, last_grad_all)
    own_taps = wide(lax.dynamic_slice_in_dim(conv_taps, dp * channels, channels, 1))

    mixer_in_w, mixer_out_w = mixer_w[:, : 3 * channels], mixer_w[:, 3 * channels : 4 * channels]
    projected = dot_nn(mixer_norm, mixer_in_w).reshape(seqs, rows, 3 * channels)
    gate_b = projected[..., :channels]
    gate_c = projected[..., channels : 2 * channels]
    conv_input = projected[..., 2 * channels :]
    conv_src = low(gate_b * conv_input)
    earlier = shifted(conv_src[:, -2:], "ctx", 1)
    extended = wide(jnp.concatenate([earlier, conv_src], 1))
    in_doc = [wide(positions >= offset)[..., None] for offset in range(3)]
    conv_sum = sum(
        own_taps[j] * extended[:, 2 - j : 2 - j + rows] * in_doc[j] for j in range(3)
    )
    conv_gated = low(gate_c * conv_sum).reshape(seqs * rows, channels)
    stream_one = stream_zero + plane_scatter(dot_nt(conv_gated, mixer_out_w))

    first_norm = plane_gather(norm_rows(stream_one, gains[1]))
    first_saved = feed_hidden(first_norm, first_w, feed_width)
    stream_two = stream_one + plane_scatter(feed_down(first_saved[2], first_w, feed_width))

    attend_norm = plane_gather(norm_rows(stream_two, gains[2]))
    qkv_w = attend_w[:, : q_cols + 2 * kv_cols]
    attend_out_w = attend_w[:, q_cols + 2 * kv_cols :]
    qkv = dot_nn(attend_norm, qkv_w).reshape(seqs, rows, -1)
    queries = qkv[..., :q_cols].reshape(seqs, rows, -1, HD)
    keys = qkv[..., q_cols : q_cols + kv_cols].reshape(seqs, rows, -1, HD)
    values = qkv[..., q_cols + kv_cols :].reshape(seqs, rows, -1, HD)
    cosine, sine = (table[:, :, None] for table in rotary_tables(positions, HD))
    query_scale, key_scale = rms_scale(queries), rms_scale(keys)
    q_gain, k_gain = wide(query_gain), wide(key_gain)
    query_rot = low(rotate(queries * query_scale * q_gain, cosine, sine))
    key_rot = low(rotate(keys * key_scale * k_gain, cosine, sine))
    kv_own = jnp.concatenate([key_rot, low(values)], -1).reshape(seqs, rows, 2 * HD)
    kv_all = jnp.stack(
        [shifted(kv_own, "ctx", distance) for distance in range(ctxs - 1, 0, -1)] + [kv_own]
    )
    query_rows = query_rot.reshape(seqs, rows, q_cols)
    context, totals = attend(query_rows, kv_all, positions)
    context = context.reshape(seqs * rows, q_cols)
    stream_three = stream_two + plane_scatter(dot_nt(context, attend_out_w))

    second_norm = plane_gather(norm_rows(stream_three, gains[3]))
    second_saved = feed_hidden(second_norm, second_w, feed_width)

    def both_halves(values):
        values = low(restore(values))
        other = lax.ppermute(values, "tensor", [(i, 1 - i) for i in range(tens)])
        lower = lax.select_n(ten, values, other)
        upper = lax.select_n(ten, other, values)
        return jnp.concatenate([lower, upper], 0)[None]

    def norm_step(upstream, stream, gain, normed_grad):
        gain_grad = jnp.sum(normed_grad * stream * rms_scale(stream), 0)
        return upstream + rms_back(stream, normed_grad * gain), gain_grad

    partial, second_grads = feed_backward(last_grad_all, second_norm, second_w, feed_width, second_saved)
    second_sums = [collect_grads(g) for g in second_grads]
    grad_three, second_gain_grad = norm_step(
        upstream, stream_three, gains[3], plane_scatter(partial)
    )
    grad_three, second_sums[2] = together(grad_three, second_sums[2])

    grad_all = plane_gather(low(grad_three))
    attend_out_grad = dot_tn(grad_all, context)
    context_grad = low(dot_nn(grad_all, attend_out_w)).reshape(seqs, rows, q_cols)
    query_acc, kv_acc = attend_back(query_rows, kv_all, positions, totals, context_grad)
    query_acc = query_acc.reshape(seqs, rows, -1, HD)
    late_hidden, kv_acc = together(second_saved[2], kv_acc)
    kv_sent = [
        shifted(kv_acc[ctxs - 1 - distance], "ctx", -distance) for distance in range(1, ctxs)
    ]
    last_branch = plane_scatter(feed_down(late_hidden, second_w, feed_width))
    last_branch, *kv_sent = together(last_branch, *kv_sent)
    kv_mine = wide(kv_acc[ctxs - 1]) + sum(wide(sent) for sent in kv_sent)
    key_grads, value_grads = kv_mine[..., :HD], kv_mine[..., HD:]
    query_norm_grad = rotate(query_acc, cosine, -sine)
    key_norm_grad = rotate(key_grads[:, :, None], cosine, -sine)
    query_gain_part = jnp.sum(query_norm_grad * queries * query_scale, (0, 1, 2))
    key_gain_part = jnp.sum(key_norm_grad * keys * key_scale, (0, 1, 2))
    query_grad = low(rms_back(queries, query_norm_grad * q_gain)).reshape(seqs * rows, -1)
    key_grad = low(rms_back(keys, key_norm_grad * k_gain)).reshape(seqs * rows, -1)
    value_grad = low(value_grads).reshape(seqs * rows, -1)
    qkv_grad = jnp.concatenate([query_grad, key_grad, value_grad], -1)
    qkv_weight_grad = dot_tn(attend_norm, qkv_grad)
    attend_grads = low(jnp.concatenate([qkv_weight_grad, attend_out_grad], -1))
    qkv_grad, attend_grads = together(qkv_grad, attend_grads)
    attend_sums = collect_grads(attend_grads)
    grad_two, attend_gain_grad = norm_step(
        grad_three,
        stream_two,
        gains[2],
        plane_scatter(dot_nt(qkv_grad, qkv_w)),
    )
    grad_two, *second_sums[:2] = together(grad_two, *second_sums[:2])

    grad_all = plane_gather(low(grad_two))
    partial, first_grads = feed_backward(grad_all, first_norm, first_w, feed_width, first_saved)
    first_sums = [collect_grads(g) for g in first_grads]
    grad_one, first_gain_grad = norm_step(grad_two, stream_one, gains[1], plane_scatter(partial))
    second_cat = jnp.concatenate(second_sums, -1)
    grad_one, attend_sums, second_cat = together(grad_one, attend_sums, second_cat)

    grad_all = plane_gather(low(grad_one))
    mixer_out_grad = dot_tn(grad_all, conv_gated)
    gated_grad = dot_nn(grad_all, mixer_out_w).reshape(seqs, rows, channels)
    gate_c_grad = low(gated_grad * conv_sum)
    sum_grad = gated_grad * gate_c
    tap_rows = []
    spread = jnp.zeros_like(extended)
    for j in range(3):
        masked = sum_grad * in_doc[j]
        tap_rows.append(jnp.sum(masked * extended[:, 2 - j : 2 - j + rows], (0, 1)))
        spread = spread + jnp.pad(own_taps[j] * masked, ((0, 0), (2 - j, j), (0, 0)))
    spread, second_cat = together(spread, second_cat)
    returned = shifted(spread[:, :2], "ctx", -1)
    second_done = by_source(send_back(second_cat))
    returned, second_done = together(returned, second_done)
    src_grad = spread[:, 2:] + jnp.pad(returned, ((0, 0), (rows - 2, 0), (0, 0)))
    proj_grad = jnp.concatenate(
        [low(src_grad * conv_input), gate_c_grad, low(src_grad * gate_b)], -1
    ).reshape(seqs * rows, 3 * channels)
    mixer_in_grad = dot_tn(mixer_norm, proj_grad)
    mixer_grads = low(jnp.concatenate([mixer_in_grad, mixer_out_grad], -1))
    mixer_grads = turn_blocks(
        mixer_grads.reshape(ctxs, seqs, part, 4 * channels).swapaxes(0, 1), 7
    ).reshape(ctxs, seqs * part, 4 * channels)
    proj_grad, mixer_grads = together(proj_grad, mixer_grads)
    mixer_sums = lax.psum_scatter(mixer_grads, "ctx", scatter_dimension=0, tiled=False)
    grad_zero, mixer_gain_grad = norm_step(
        grad_one,
        stream_zero,
        gains[0],
        plane_scatter(dot_nt(proj_grad, mixer_in_w)),
    )
    hidden_out = both_halves(stream_three + last_branch)
    hidden_grad = both_halves(grad_zero)

    gain_rows = restore(
        jnp.stack([mixer_gain_grad, first_gain_grad, attend_gain_grad, second_gain_grad])
    )
    taps_part = lax.dynamic_update_slice(
        jnp.zeros((tens, 3, channels * seqs), jnp.float32),
        jnp.stack(tap_rows)[None],
        (ten, 0, dp * channels),
    )
    small = jnp.concatenate(
        [gain_rows.reshape(-1), query_gain_part, key_gain_part, taps_part.reshape(-1)]
    )
    first_cat = jnp.concatenate(first_sums + [attend_sums], -1)
    first_parts = send_back(first_cat)
    small, mixer_sums, *first_parts = together(small, mixer_sums, *first_parts)
    first_done = by_source(first_parts)
    mixer_done = wide(mixer_sums).reshape(seqs, part, -1).swapaxes(0, 1)
    small = small_sum(small, 5)
    gain_sums = lax.dynamic_slice_in_dim(
        small[: 4 * width].reshape(4, width), (dp * ctxs + ctx) * part, part, 1
    )
    query_gain_grad = small[4 * width : 4 * width + HD]
    key_gain_grad = small[4 * width + HD : 4 * width + 2 * HD]
    taps_grad = lax.dynamic_index_in_dim(
        small[4 * width + 2 * HD :].reshape(tens, 3, channels * seqs), ten, 0, keepdims=False
    )

    def columns(done, start, count):
        return done[:, :, start : start + count].reshape(part, -1)

    def feed_columns(done, number):
        return columns(done, number * feed_width, feed_width)[:, :units]

    attend_at = 3 * feed_width

    return (
        hidden_out,
        hidden_grad,
        gain_sums[0],
        jnp.stack([columns(mixer_done, k * channels, channels) for k in range(3)]),
        taps_grad,
        columns(mixer_done, 3 * channels, channels).T,
        gain_sums[1],
        feed_columns(first_done, 0),
        feed_columns(first_done, 1),
        feed_columns(first_done, 2).T,
        gain_sums[2],
        columns(first_done, attend_at, q_cols),
        columns(first_done, attend_at + q_cols, kv_cols),
        columns(first_done, attend_at + q_cols + kv_cols, kv_cols),
        query_gain_grad,
        key_gain_grad,
        columns(first_done, attend_at + q_cols + 2 * kv_cols, q_cols).T,
        gain_sums[3],
        feed_columns(second_done, 0),
        feed_columns(second_done, 1),
        feed_columns(second_done, 2).T,
    )


def solution(mesh):
    rows = P("dp", "ctx", None)
    gain = P(("dp", "ctx"))
    into = P(("dp", "ctx"), "tensor")
    out = P("tensor", ("dp", "ctx"))
    thrice = P(None, ("dp", "ctx"), "tensor")
    taps = P(None, "tensor")
    weights = (
        (gain, thrice, taps, out, gain, into, into, out)
        + (gain, into, into, into, P(), P(), out)
        + (gain, into, into, out)
    )
    return jax.shard_map(
        shards,
        mesh=mesh,
        in_specs=(rows, P("dp", "ctx")) + weights + (rows,),
        out_specs=(rows, rows) + weights,
        check_vma=False,
    )
```

```python
import functools
import math

import jax
import jax.numpy as jnp
from jax import lax
from jax.experimental import pallas as pl
from jax.experimental.pallas import tpu as pltpu
from jax.sharding import PartitionSpec as P

H = 24
KV = 8
HD = 64
GROUPS = H // KV
LANES = 128

epsilon = 1e-05
MESH = pl.DeviceIdType.MESH


def plane_place():
    dp = lax.axis_index("dp")
    ten = lax.axis_index("tensor")
    core = lax.rem(dp, 2)
    across = lax.rem(dp + 2, 4)
    twin = dp + 1 - 2 * core
    return dp, ten, core, across, twin


def greet(dp, ten, across, twin):
    barrier = pltpu.get_barrier_semaphore()
    pl.semaphore_signal(barrier, 1, device_id={"dp": across}, device_id_type=MESH)
    pl.semaphore_signal(barrier, 1, device_id={"tensor": 1 - ten}, device_id_type=MESH)
    pl.semaphore_signal(barrier, 1, device_id={"dp": twin}, device_id_type=MESH)
    pl.semaphore_wait(barrier, 3)


def remote(src, dst, send, recv, place):
    return pltpu.make_async_remote_copy(
        src_ref=src,
        dst_ref=dst,
        send_sem=send,
        recv_sem=recv,
        device_id=place,
        device_id_type=MESH,
    )


def gather_kernel(x_ref, o_ref, own_sem, send, recv):
    dp, ten, core, across, twin = plane_place()
    greet(dp, ten, across, twin)
    to_across = {"dp": across, "tensor": ten}
    to_side = {"dp": dp, "tensor": 1 - ten}
    to_twin = {"dp": twin, "tensor": ten}
    own = dp * 2 + ten
    first = (across * (1 - core) + dp * core) * 2 + ten * (1 - core) + (1 - ten) * core
    other = (dp * (1 - core) + across * core) * 2 + (1 - ten) * (1 - core) + ten * core
    onward = {
        "dp": dp * (1 - core) + across * core,
        "tensor": (1 - ten) * (1 - core) + ten * core,
    }
    far = across * 2 + 1 - ten

    def move(src, slot, number, place):
        copy = remote(src, o_ref.at[slot], send.at[number], recv.at[slot], place)
        copy.start()
        return copy

    copies = [
        move(x_ref, own, 0, to_across),
        move(x_ref, own, 1, to_side),
        move(x_ref, own, 2, to_twin),
    ]
    local = pltpu.make_async_copy(x_ref, o_ref.at[own], own_sem)
    local.start()

    def arrived(slot):
        remote(x_ref, o_ref.at[slot], send.at[0], recv.at[slot], to_twin).wait_recv()

    arrived(first)
    copies.append(move(o_ref.at[first], first, 3, onward))
    copies.append(move(o_ref.at[first], first, 4, to_twin))
    arrived(other)
    copies.append(move(o_ref.at[other], other, 5, to_twin))
    arrived(far)
    copies.append(move(o_ref.at[far], far, 6, to_twin))
    twin_across = lax.rem(twin + 2, 4)
    for there in (twin, twin_across):
        for side in range(2):
            arrived(there * 2 + side)
    local.wait()
    for copy in copies:
        copy.wait_send()


def plane_gather(block):
    rows, width = block.shape
    slots = lax.axis_size("dp") * lax.axis_size("tensor")
    gathered = pl.pallas_call(
        gather_kernel,
        out_shape=jax.ShapeDtypeStruct((slots, rows, width), block.dtype),
        in_specs=[pl.BlockSpec(memory_space=pltpu.VMEM)],
        out_specs=pl.BlockSpec(memory_space=pl.ANY),
        scratch_shapes=[
            pltpu.SemaphoreType.DMA,
            pltpu.SemaphoreType.DMA((7,)),
            pltpu.SemaphoreType.DMA((8,)),
        ],
        compiler_params=pltpu.CompilerParams(
            collective_id=1, has_side_effects=True, vmem_limit_bytes=16 << 20
        ),
    )(block)
    return gathered.reshape(slots * rows, width)


def scatter_kernel(p_ref, o_ref, mine, theirs, out_box, in_box, load, send, recv):
    dp, ten, core, across, twin = plane_place()
    greet(dp, ten, across, twin)
    twin_across = lax.rem(twin + 2, 4)
    to_twin = {"dp": twin, "tensor": ten}
    sides = (ten, 1 - ten, ten, 1 - ten)
    home = (dp, dp, across, across)
    away = (twin, twin, twin_across, twin_across)
    order = (3, 1, 2, 0)
    loads = {}
    gifts = {}
    for rel in order:
        gifts[rel] = remote(
            p_ref.at[away[rel] * 2 + sides[rel]],
            theirs.at[rel],
            send.at[rel],
            recv.at[rel],
            to_twin,
        )
        gifts[rel].start()
        loads[rel] = pltpu.make_async_copy(
            p_ref.at[home[rel] * 2 + sides[rel]], mine.at[rel], load.at[rel]
        )
        loads[rel].start()
    direct = 1 + core
    relayed = 2 - core
    to_direct = {
        "dp": dp * (1 - core) + across * core,
        "tensor": (1 - ten) * (1 - core) + ten * core,
    }
    to_relayed = {
        "dp": across * (1 - core) + dp * core,
        "tensor": ten * (1 - core) + (1 - ten) * core,
    }

    def total(rel):
        return mine[rel].astype(jnp.float32) + theirs[rel].astype(jnp.float32)

    def post(number, value, place):
        out_box[number] = value.astype(out_box.dtype)
        copy = remote(
            out_box.at[number], in_box.at[number], send.at[4 + number], recv.at[4 + number], place
        )
        copy.start()
        return copy

    loads[3].wait()
    gifts[3].wait_recv()
    relay = post(0, total(3), to_direct)
    for rel in (1, 2):
        loads[rel].wait()
        gifts[rel].wait_recv()
    straight = post(1, total(direct), to_direct)
    relay.wait_recv()
    bent = post(2, total(relayed) + in_box[0].astype(jnp.float32), to_relayed)
    loads[0].wait()
    gifts[0].wait_recv()
    partial = total(0)
    straight.wait_recv()
    partial = partial + in_box[1].astype(jnp.float32)
    bent.wait_recv()
    o_ref[...] = partial + in_box[2].astype(jnp.float32)
    for rel in order:
        gifts[rel].wait_send()
    for copy in (relay, straight, bent):
        copy.wait_send()


def plane_scatter(partial):
    slots = lax.axis_size("dp") * lax.axis_size("tensor")
    rows, width = partial.shape[0] // slots, partial.shape[1]
    block = (rows, width)
    return pl.pallas_call(
        scatter_kernel,
        out_shape=jax.ShapeDtypeStruct(block, jnp.float32),
        in_specs=[pl.BlockSpec(memory_space=pl.ANY)],
        out_specs=pl.BlockSpec(memory_space=pltpu.VMEM),
        scratch_shapes=[
            pltpu.VMEM((4,) + block, jnp.bfloat16),
            pltpu.VMEM((4,) + block, jnp.bfloat16),
            pltpu.VMEM((3,) + block, jnp.bfloat16),
            pltpu.VMEM((3,) + block, jnp.bfloat16),
            pltpu.SemaphoreType.DMA((4,)),
            pltpu.SemaphoreType.DMA((7,)),
            pltpu.SemaphoreType.DMA((7,)),
        ],
        compiler_params=pltpu.CompilerParams(
            collective_id=2, has_side_effects=True, vmem_limit_bytes=24 << 20
        ),
    )(partial.astype(jnp.bfloat16).reshape((slots,) + block))


def swap_kernel(x_ref, o_ref, own_sem, send, recv):
    dp = lax.axis_index("dp")
    ten = lax.axis_index("tensor")
    barrier = pltpu.get_barrier_semaphore()
    for step in (1, 2, 3):
        pl.semaphore_signal(
            barrier,
            1,
            device_id={"dp": lax.rem(dp + step, 4), "tensor": ten},
            device_id_type=MESH,
        )
    pl.semaphore_wait(barrier, 3)
    copies = []
    for step in (2, 1, 3):
        there = lax.rem(dp + step, 4)
        copy = remote(
            x_ref.at[there],
            o_ref.at[dp],
            send.at[step],
            recv.at[step],
            {"dp": there, "tensor": ten},
        )
        copy.start()
        copies.append(copy)
    local = pltpu.make_async_copy(x_ref.at[dp], o_ref.at[dp], own_sem)
    local.start()
    for copy in copies:
        copy.wait()
    local.wait()


def turn_kernel(x_ref, o_ref, own_sem, send, recv):
    dp = lax.axis_index("dp")
    ten = lax.axis_index("tensor")
    barrier = pltpu.get_barrier_semaphore()
    for step in (1, 2, 3):
        pl.semaphore_signal(
            barrier,
            1,
            device_id={"dp": lax.rem(dp + step, 4), "tensor": ten},
            device_id_type=MESH,
        )
    pl.semaphore_wait(barrier, 3)
    copies = []
    for step in (2, 1, 3):
        there = lax.rem(dp + step, 4)
        copy = remote(
            x_ref.at[there],
            o_ref.at[:, dp],
            send.at[step],
            recv.at[step],
            {"dp": there, "tensor": ten},
        )
        copy.start()
        copies.append(copy)
    local = pltpu.make_async_copy(x_ref.at[dp], o_ref.at[:, dp], own_sem)
    local.start()
    for copy in copies:
        copy.wait()
    local.wait()


def turn_blocks(blocks, number):
    shape = (blocks.shape[1], blocks.shape[0]) + blocks.shape[2:]
    return pl.pallas_call(
        turn_kernel,
        out_shape=jax.ShapeDtypeStruct(shape, blocks.dtype),
        in_specs=[pl.BlockSpec(memory_space=pltpu.VMEM)],
        out_specs=pl.BlockSpec(memory_space=pl.ANY),
        scratch_shapes=[
            pltpu.SemaphoreType.DMA,
            pltpu.SemaphoreType.DMA((4,)),
            pltpu.SemaphoreType.DMA((4,)),
        ],
        compiler_params=pltpu.CompilerParams(
            collective_id=number, has_side_effects=True, vmem_limit_bytes=16 << 20
        ),
    )(blocks)


def swap_blocks(blocks, number):
    return pl.pallas_call(
        swap_kernel,
        out_shape=jax.ShapeDtypeStruct(blocks.shape, blocks.dtype),
        in_specs=[pl.BlockSpec(memory_space=pltpu.VMEM)],
        out_specs=pl.BlockSpec(memory_space=pl.ANY),
        scratch_shapes=[
            pltpu.SemaphoreType.DMA,
            pltpu.SemaphoreType.DMA((4,)),
            pltpu.SemaphoreType.DMA((4,)),
        ],
        compiler_params=pltpu.CompilerParams(
            collective_id=number, has_side_effects=True, vmem_limit_bytes=16 << 20
        ),
    )(blocks)


def send_back(blocks):
    dp = lax.axis_index("dp")
    devices = range(lax.axis_size("dp"))
    parts = [lax.dynamic_index_in_dim(blocks, dp, 0, keepdims=False)]
    for flip in (1, 2, 3):
        sent = lax.dynamic_index_in_dim(blocks, dp ^ flip, 0, keepdims=False)
        parts.append(lax.ppermute(sent, "dp", [(i, i ^ flip) for i in devices]))
    return parts


def by_source(parts, start, count):
    dp = lax.axis_index("dp")
    devices = range(lax.axis_size("dp"))
    cut = [part[:, start : start + count] for part in parts]
    return jnp.concatenate(
        [wide(lax.select_n(dp, *(cut[j ^ i] for i in devices))) for j in devices], 1
    )


def from_all_dp(block):
    dp = lax.axis_index("dp")
    devices = range(lax.axis_size("dp"))
    parts = [block] + [
        lax.ppermute(block, "dp", [(i, i ^ flip) for i in devices]) for flip in (1, 2, 3)
    ]
    return jnp.concatenate([lax.select_n(dp, *(parts[j ^ i] for i in devices)) for j in devices], 0)


def together(*values):
    return lax.optimization_barrier(values)


def small_sum_kernel(x_ref, o_ref, plane_box, plane_sum, line_box, send, recv, line_send, line_recv):
    dp, ten, ctx = (lax.axis_index(name) for name in ("dp", "tensor", "ctx"))
    dps, tens, ctxs = (lax.axis_size(name) for name in ("dp", "tensor", "ctx"))
    slots = dps * tens
    own = dp * tens + ten
    barrier = pltpu.get_barrier_semaphore()

    def plane_peer(step):
        slot = lax.rem(own + step, slots)
        return {"dp": slot // tens, "tensor": lax.rem(slot, tens), "ctx": ctx}

    def line_peer(step):
        return {"dp": dp, "tensor": ten, "ctx": lax.rem(ctx + step, ctxs)}

    for step in range(1, slots):
        pl.semaphore_signal(barrier, 1, device_id=plane_peer(step), device_id_type=MESH)
    for step in range(1, ctxs):
        pl.semaphore_signal(barrier, 1, device_id=line_peer(step), device_id_type=MESH)
    pl.semaphore_wait(barrier, slots + ctxs - 2)
    copies = []
    for step in range(1, slots):
        copy = remote(
            x_ref, plane_box.at[step], send.at[step], recv.at[step], plane_peer(step)
        )
        copy.start()
        copies.append(copy)
    total = x_ref[...]
    for copy in copies:
        copy.wait_recv()
    for step in range(1, slots):
        total = total + plane_box[step]
    plane_sum[...] = total
    lines = []
    for step in range(1, ctxs):
        copy = remote(
            plane_sum, line_box.at[step], line_send.at[step], line_recv.at[step], line_peer(step)
        )
        copy.start()
        lines.append(copy)
    for copy in lines:
        copy.wait_recv()
    for step in range(1, ctxs):
        total = total + line_box[step]
    o_ref[...] = total
    for copy in copies + lines:
        copy.wait_send()


def small_gather_kernel(x_ref, o_ref, own_sem, send, recv, line_send, line_recv):
    dp, ten, ctx = (lax.axis_index(name) for name in ("dp", "tensor", "ctx"))
    dps, ctxs = (lax.axis_size(name) for name in ("dp", "ctx"))
    barrier = pltpu.get_barrier_semaphore()

    def dp_peer(step):
        return {"dp": lax.rem(dp + step, dps), "tensor": ten, "ctx": ctx}

    def ctx_peer(step):
        return {"dp": dp, "tensor": ten, "ctx": lax.rem(ctx + step, ctxs)}

    for step in range(1, dps):
        pl.semaphore_signal(barrier, 1, device_id=dp_peer(step), device_id_type=MESH)
    for step in range(1, ctxs):
        pl.semaphore_signal(barrier, 1, device_id=ctx_peer(step), device_id_type=MESH)
    pl.semaphore_wait(barrier, dps + ctxs - 2)
    copies = []
    for step in range(1, dps):
        copy = remote(x_ref, o_ref.at[ctx, dp], send.at[step], recv.at[step], dp_peer(step))
        copy.start()
        copies.append(copy)
    local = pltpu.make_async_copy(x_ref, o_ref.at[ctx, dp], own_sem)
    local.start()
    local.wait()
    for copy in copies:
        copy.wait()
    lines = []
    for step in range(1, ctxs):
        copy = remote(
            o_ref.at[ctx], o_ref.at[ctx], line_send.at[step], line_recv.at[step], ctx_peer(step)
        )
        copy.start()
        lines.append(copy)
    for copy in lines:
        copy.wait()


def small_gather(block, number):
    dps, ctxs = lax.axis_size("dp"), lax.axis_size("ctx")
    return pl.pallas_call(
        small_gather_kernel,
        out_shape=jax.ShapeDtypeStruct((ctxs, dps) + block.shape, block.dtype),
        in_specs=[pl.BlockSpec(memory_space=pltpu.VMEM)],
        out_specs=pl.BlockSpec(memory_space=pltpu.VMEM),
        scratch_shapes=[
            pltpu.SemaphoreType.DMA,
            pltpu.SemaphoreType.DMA((dps,)),
            pltpu.SemaphoreType.DMA((dps,)),
            pltpu.SemaphoreType.DMA((ctxs,)),
            pltpu.SemaphoreType.DMA((ctxs,)),
        ],
        compiler_params=pltpu.CompilerParams(
            collective_id=number, has_side_effects=True, vmem_limit_bytes=16 << 20
        ),
    )(block)


def small_sum(values, number):
    count = values.size
    rows = -(-count // (8 * LANES)) * 8
    block = jnp.pad(values.reshape(-1), (0, rows * LANES - count)).reshape(rows, LANES)
    slots = lax.axis_size("dp") * lax.axis_size("tensor")
    ctxs = lax.axis_size("ctx")
    total = pl.pallas_call(
        small_sum_kernel,
        out_shape=jax.ShapeDtypeStruct(block.shape, jnp.float32),
        in_specs=[pl.BlockSpec(memory_space=pltpu.VMEM)],
        out_specs=pl.BlockSpec(memory_space=pltpu.VMEM),
        scratch_shapes=[
            pltpu.VMEM((slots,) + block.shape, jnp.float32),
            pltpu.VMEM(block.shape, jnp.float32),
            pltpu.VMEM((ctxs,) + block.shape, jnp.float32),
            pltpu.SemaphoreType.DMA((slots,)),
            pltpu.SemaphoreType.DMA((slots,)),
            pltpu.SemaphoreType.DMA((ctxs,)),
            pltpu.SemaphoreType.DMA((ctxs,)),
        ],
        compiler_params=pltpu.CompilerParams(
            collective_id=number, has_side_effects=True, vmem_limit_bytes=16 << 20
        ),
    )(block)
    return total.reshape(-1)[:count]


def rms_scale(values):
    return lax.rsqrt(jnp.mean(values * values, -1, keepdims=True) + epsilon)


def rms_back(values, upstream):
    row_scale = rms_scale(values)
    normed = values * row_scale
    return row_scale * (upstream - normed * jnp.mean(upstream * normed, -1, keepdims=True))


def low(values):
    return values.astype(jnp.bfloat16)


def wide(values):
    return values.astype(jnp.float32)


def dot_nn(left, right):
    return lax.dot_general(left, right, (((1,), (0,)), ((), ())), preferred_element_type=jnp.float32)


def dot_nt(left, right):
    return lax.dot_general(left, right, (((1,), (1,)), ((), ())), preferred_element_type=jnp.float32)


def dot_tn(left, right):
    return lax.dot_general(left, right, (((0,), (0,)), ((), ())), preferred_element_type=jnp.float32)


def shifted(block, axis, distance):
    devices = range(lax.axis_size(axis))
    route = [(i - distance, i) for i in devices if i - distance in devices]
    return lax.ppermute(block, axis, route)


def rotary_tables(positions, head_dim):
    half_dim = head_dim // 2
    freqs = jnp.exp(-math.log(1000000.0) * 2.0 * jnp.arange(half_dim, dtype=jnp.float32) / head_dim)
    angles = wide(positions)[..., None] * freqs
    return (jnp.cos(angles), jnp.sin(angles))


def rotate(values, cosine, sine):
    half_dim = values.shape[-1] // 2
    first, second = values[..., :half_dim], values[..., half_dim:]
    return jnp.concatenate([first * cosine - second * sine, second * cosine + first * sine], -1)


def visible(pos_ref, rows, key_rows):
    query_at = lax.broadcasted_iota(jnp.int32, (rows, key_rows), 0) + (key_rows - rows)
    key_at = lax.broadcasted_iota(jnp.int32, (rows, key_rows), 1)
    return (key_at <= query_at) & (key_at >= query_at - pos_ref[0])


def attend_kernel(q_ref, kv_ref, pos_ref, context_ref, lse_ref):
    rows = q_ref.shape[1]
    key_rows = kv_ref.shape[0] * rows
    both = kv_ref[...].reshape(key_rows, 2 * HD)
    keys, values = both[:, :HD], both[:, HD:]
    allowed = visible(pos_ref, rows, key_rows)
    contexts, totals = [], []
    for head in range(GROUPS):
        query = q_ref[0, :, head * HD : (head + 1) * HD]
        scores = jnp.where(allowed, dot_nt(query, keys) * (1.0 / math.sqrt(HD)), -1e30)
        top = jnp.max(scores, -1, keepdims=True)
        weights = jnp.exp(scores - top)
        total = jnp.sum(weights, -1, keepdims=True)
        contexts.append(low(dot_nn(low(weights * (1.0 / total)), values)))
        totals.append(top + jnp.log(total))
    context_ref[0] = jnp.concatenate(contexts, -1)
    lse_ref[0] = jnp.concatenate(totals + [jnp.zeros_like(totals[0])] * (8 - GROUPS), -1)


def attend_back_kernel(q_ref, kv_ref, pos_ref, lse_ref, grad_ref, dq_ref, dkv_ref):
    rows = q_ref.shape[1]
    key_rows = kv_ref.shape[0] * rows
    both = kv_ref[...].reshape(key_rows, 2 * HD)
    keys, values = both[:, :HD], both[:, HD:]
    allowed = visible(pos_ref, rows, key_rows)
    root = 1.0 / math.sqrt(HD)
    query_grads = []
    key_grad = jnp.zeros((key_rows, HD), jnp.float32)
    value_grad = jnp.zeros((key_rows, HD), jnp.float32)
    for head in range(GROUPS):
        query = q_ref[0, :, head * HD : (head + 1) * HD]
        grad = grad_ref[0, :, head * HD : (head + 1) * HD]
        scores = dot_nt(query, keys) * root - lse_ref[0, :, head : head + 1]
        probs = jnp.where(allowed, jnp.exp(jnp.where(allowed, scores, 0.0)), 0.0)
        prob_grad = dot_nt(grad, values)
        delta = jnp.sum(probs * prob_grad, -1, keepdims=True)
        score_grad = low(probs * (prob_grad - delta))
        query_grads.append(dot_nn(score_grad, keys) * root)
        key_grad = key_grad + dot_tn(score_grad, query)
        value_grad = value_grad + dot_tn(low(probs), grad)
    dq_ref[0] = jnp.concatenate(query_grads, -1)
    whole = low(jnp.concatenate([key_grad * root, value_grad], -1))
    dkv_ref[...] = whole.reshape(dkv_ref.shape)


def attend_specs(seqs, rows, parts):
    by_seq = lambda width: pl.BlockSpec((1, rows, width), lambda s: (s, 0, 0))
    over_keys = pl.BlockSpec((parts, 1, rows, 2 * HD), lambda s: (0, s, 0, 0))
    return by_seq, over_keys


def attend(queries, kv_all, positions):
    seqs, rows, width = queries.shape
    by_seq, over_keys = attend_specs(seqs, rows, kv_all.shape[0])
    return pl.pallas_call(
        attend_kernel,
        grid=(seqs,),
        out_shape=(
            jax.ShapeDtypeStruct(queries.shape, jnp.bfloat16),
            jax.ShapeDtypeStruct((seqs, rows, 8), jnp.float32),
        ),
        in_specs=[by_seq(width), over_keys, by_seq(1)],
        out_specs=(by_seq(width), by_seq(8)),
        compiler_params=pltpu.CompilerParams(vmem_limit_bytes=56 << 20),
    )(queries, kv_all, positions[..., None])


def attend_back(queries, kv_all, positions, totals, grads):
    seqs, rows, width = queries.shape
    by_seq, over_keys = attend_specs(seqs, rows, kv_all.shape[0])
    return pl.pallas_call(
        attend_back_kernel,
        grid=(seqs,),
        out_shape=(
            jax.ShapeDtypeStruct(queries.shape, jnp.float32),
            jax.ShapeDtypeStruct(kv_all.shape, jnp.bfloat16),
        ),
        in_specs=[by_seq(width), over_keys, by_seq(1), by_seq(8), by_seq(width)],
        out_specs=(by_seq(width), over_keys),
        compiler_params=pltpu.CompilerParams(vmem_limit_bytes=56 << 20),
    )(queries, kv_all, positions[..., None], totals, grads)


def column_blocks(weight, count, width):
    rows, columns = weight.shape
    weight = jnp.pad(weight, ((0, 0), (0, count * width - columns)))
    return weight.reshape(rows, count, width).transpose(1, 0, 2)


def spread_weights(blocks, number):
    mine = swap_blocks(blocks, number)
    whole = lax.all_gather(mine, "ctx", axis=0, tiled=False)
    return whole.reshape(-1, whole.shape[-1])


def collect_grads(grad):
    ctx, count = lax.axis_size("ctx"), lax.axis_size("dp")
    grad = low(grad).reshape(ctx, -1, grad.shape[-1])
    summed = lax.psum_scatter(grad, "ctx", scatter_dimension=0, tiled=False)
    return summed.reshape(count, -1, summed.shape[-1])


def feed_hidden(normed, weights, width):
    both = dot_nn(normed, weights[:, : 2 * width])
    gate, lift = both[:, :width], both[:, width:]
    return gate, lift, low(jax.nn.silu(gate) * lift)


def feed_down(hidden, weights, width):
    return low(dot_nt(hidden, weights[:, 2 * width :]))


def feed_backward(grad_all, normed, weights, width, saved):
    gate, lift, hidden = saved
    down_grad, grad_all = together(low(dot_tn(grad_all, hidden)), grad_all)
    hidden_grad = dot_nn(grad_all, weights[:, 2 * width :])
    sig = jax.nn.sigmoid(gate)
    gate_grad = low(hidden_grad * lift * sig * (1.0 + gate * (1.0 - sig)))
    lift_grad = low(hidden_grad * gate * sig)
    gate_weight_grad = low(dot_tn(normed, gate_grad))
    lift_weight_grad = low(dot_tn(normed, lift_grad))
    gate_grad, lift_grad, gate_weight_grad, lift_weight_grad = together(
        gate_grad, lift_grad, gate_weight_grad, lift_weight_grad
    )
    partial = dot_nt(gate_grad, weights[:, :width]) + dot_nt(
        lift_grad, weights[:, width : 2 * width]
    )
    return partial, (gate_weight_grad, lift_weight_grad, down_grad)


def shards(
    hidden_in,
    doc_pos,
    mixer_gain,
    mixer_in,
    conv_taps,
    mixer_out,
    feed_first,
    gate_first,
    lift_first,
    down_first,
    attend_gain,
    query_proj,
    key_proj,
    value_proj,
    query_gain,
    key_gain,
    attend_out,
    feed_second,
    gate_second,
    lift_second,
    down_second,
    output_grad,
):
    dp, ten, ctx = (lax.axis_index(name) for name in ("dp", "tensor", "ctx"))
    seqs, tens, ctxs = (lax.axis_size(name) for name in ("dp", "tensor", "ctx"))
    rows, width = hidden_in.shape[1], hidden_in.shape[2]
    own_rows = rows // tens
    part = mixer_gain.shape[0]
    channels = mixer_in.shape[2] // seqs
    units = gate_first.shape[1]
    feed_width = -(-units // (seqs * LANES)) * LANES

    def regroup(values):
        lead = values.shape[:-1]
        return values.reshape(lead + (seqs, ctxs, part)).swapaxes(-3, -2).reshape(lead + (width,))

    def restore(values):
        lead = values.shape[:-1]
        return values.reshape(lead + (ctxs, seqs, part)).swapaxes(-3, -2).reshape(lead + (width,))

    def own_half(values):
        return regroup(lax.dynamic_slice_in_dim(values[0], ten * own_rows, own_rows, 0))

    stream_zero = wide(own_half(hidden_in))
    upstream = wide(own_half(output_grad))
    last_grad_all = plane_gather(low(upstream))

    def norm_rows(stream, gain):
        return low(stream * rms_scale(stream) * gain)

    mixer_blocks = jnp.concatenate(
        [column_blocks(mixer_in[k], seqs, channels) for k in range(3)]
        + [column_blocks(mixer_out.T, seqs, channels)],
        -1,
    )
    mixer_w = spread_weights(mixer_blocks, 3)
    own_gains = wide(jnp.stack([mixer_gain, feed_first, attend_gain, feed_second]))
    own_gains = jnp.pad(own_gains, ((0, 4), (0, -part % LANES)))
    gains = small_gather(own_gains, 8)[:, :, :4, :part]
    gains = gains.transpose(2, 0, 1, 3).reshape(4, width)
    first_blocks = jnp.concatenate(
        [column_blocks(w, seqs, feed_width) for w in (gate_first, lift_first, down_first.T)], -1
    )
    first_w = spread_weights(first_blocks, 4)
    q_cols, kv_cols = query_proj.shape[1] // seqs, key_proj.shape[1] // seqs
    attend_blocks = jnp.concatenate(
        [
            column_blocks(query_proj, seqs, q_cols),
            column_blocks(key_proj, seqs, kv_cols),
            column_blocks(value_proj, seqs, kv_cols),
            column_blocks(attend_out.T, seqs, q_cols),
        ],
        -1,
    )
    attend_w = spread_weights(attend_blocks, 6)
    second_blocks = jnp.concatenate(
        [column_blocks(w, seqs, feed_width) for w in (gate_second, lift_second, down_second.T)], -1
    )
    second_w = spread_weights(second_blocks, 4)

    positions = from_all_dp(doc_pos)
    mixer_norm = plane_gather(norm_rows(stream_zero, gains[0]))
    mixer_w, mixer_norm, last_grad_all = together(mixer_w, mixer_norm, last_grad_all)
    own_taps = wide(lax.dynamic_slice_in_dim(conv_taps, dp * channels, channels, 1))

    mixer_in_w, mixer_out_w = mixer_w[:, : 3 * channels], mixer_w[:, 3 * channels : 4 * channels]
    projected = dot_nn(mixer_norm, mixer_in_w).reshape(seqs, rows, 3 * channels)
    gate_b = projected[..., :channels]
    gate_c = projected[..., channels : 2 * channels]
    conv_input = projected[..., 2 * channels :]
    conv_src = low(gate_b * conv_input)
    earlier = shifted(conv_src[:, -2:], "ctx", 1)
    extended = wide(jnp.concatenate([earlier, conv_src], 1))
    in_doc = [wide(positions >= offset)[..., None] for offset in range(3)]
    conv_sum = sum(
        own_taps[j] * extended[:, 2 - j : 2 - j + rows] * in_doc[j] for j in range(3)
    )
    conv_gated = low(gate_c * conv_sum).reshape(seqs * rows, channels)
    stream_one = stream_zero + plane_scatter(dot_nt(conv_gated, mixer_out_w))

    first_norm = plane_gather(norm_rows(stream_one, gains[1]))
    first_saved = feed_hidden(first_norm, first_w, feed_width)
    stream_two = stream_one + plane_scatter(feed_down(first_saved[2], first_w, feed_width))

    attend_norm = plane_gather(norm_rows(stream_two, gains[2]))
    qkv_w = attend_w[:, : q_cols + 2 * kv_cols]
    attend_out_w = attend_w[:, q_cols + 2 * kv_cols :]
    qkv = dot_nn(attend_norm, qkv_w).reshape(seqs, rows, -1)
    queries = qkv[..., :q_cols].reshape(seqs, rows, -1, HD)
    keys = qkv[..., q_cols : q_cols + kv_cols].reshape(seqs, rows, -1, HD)
    values = qkv[..., q_cols + kv_cols :].reshape(seqs, rows, -1, HD)
    cosine, sine = (table[:, :, None] for table in rotary_tables(positions, HD))
    query_scale, key_scale = rms_scale(queries), rms_scale(keys)
    q_gain, k_gain = wide(query_gain), wide(key_gain)
    query_rot = low(rotate(queries * query_scale * q_gain, cosine, sine))
    key_rot = low(rotate(keys * key_scale * k_gain, cosine, sine))
    kv_own = jnp.concatenate([key_rot, low(values)], -1).reshape(seqs, rows, 2 * HD)
    kv_all = jnp.stack(
        [shifted(kv_own, "ctx", distance) for distance in range(ctxs - 1, 0, -1)] + [kv_own]
    )
    query_rows = query_rot.reshape(seqs, rows, q_cols)
    context, totals = attend(query_rows, kv_all, positions)
    context = context.reshape(seqs * rows, q_cols)
    stream_three = stream_two + plane_scatter(dot_nt(context, attend_out_w))

    second_norm = plane_gather(norm_rows(stream_three, gains[3]))
    second_saved = feed_hidden(second_norm, second_w, feed_width)

    def both_halves(values):
        values = low(restore(values))
        other = lax.ppermute(values, "tensor", [(i, 1 - i) for i in range(tens)])
        lower = lax.select_n(ten, values, other)
        upper = lax.select_n(ten, other, values)
        return jnp.concatenate([lower, upper], 0)[None]

    def norm_step(upstream, stream, gain, normed_grad):
        gain_grad = jnp.sum(normed_grad * stream * rms_scale(stream), 0)
        return upstream + rms_back(stream, normed_grad * gain), gain_grad

    partial, second_grads = feed_backward(last_grad_all, second_norm, second_w, feed_width, second_saved)
    second_sums = [collect_grads(g) for g in second_grads]
    grad_three, second_gain_grad = norm_step(
        upstream, stream_three, gains[3], plane_scatter(partial)
    )

    grad_all = plane_gather(low(grad_three))
    grad_all, second_sums[2] = together(grad_all, second_sums[2])
    attend_out_grad = dot_tn(grad_all, context)
    context_grad = low(dot_nn(grad_all, attend_out_w)).reshape(seqs, rows, q_cols)
    query_acc, kv_acc = attend_back(query_rows, kv_all, positions, totals, context_grad)
    query_acc = query_acc.reshape(seqs, rows, -1, HD)
    late_hidden, kv_acc = together(second_saved[2], kv_acc)
    kv_sent = [
        shifted(kv_acc[ctxs - 1 - distance], "ctx", -distance) for distance in range(1, ctxs)
    ]
    last_branch = plane_scatter(feed_down(late_hidden, second_w, feed_width))
    last_branch, *kv_sent = together(last_branch, *kv_sent)
    kv_mine = wide(kv_acc[ctxs - 1]) + sum(wide(sent) for sent in kv_sent)
    key_grads, value_grads = kv_mine[..., :HD], kv_mine[..., HD:]
    query_norm_grad = rotate(query_acc, cosine, -sine)
    key_norm_grad = rotate(key_grads[:, :, None], cosine, -sine)
    query_gain_part = jnp.sum(query_norm_grad * queries * query_scale, (0, 1, 2))
    key_gain_part = jnp.sum(key_norm_grad * keys * key_scale, (0, 1, 2))
    query_grad = low(rms_back(queries, query_norm_grad * q_gain)).reshape(seqs * rows, -1)
    key_grad = low(rms_back(keys, key_norm_grad * k_gain)).reshape(seqs * rows, -1)
    value_grad = low(value_grads).reshape(seqs * rows, -1)
    qkv_grad = jnp.concatenate([query_grad, key_grad, value_grad], -1)
    qkv_weight_grad = dot_tn(attend_norm, qkv_grad)
    attend_grads = low(jnp.concatenate([qkv_weight_grad, attend_out_grad], -1))
    qkv_grad, attend_grads = together(qkv_grad, attend_grads)
    attend_sums = collect_grads(attend_grads)
    grad_two, attend_gain_grad = norm_step(
        grad_three,
        stream_two,
        gains[2],
        plane_scatter(dot_nt(qkv_grad, qkv_w)),
    )
    grad_two, *second_sums = together(grad_two, *second_sums)

    grad_all = plane_gather(low(grad_two))
    partial, first_grads = feed_backward(grad_all, first_norm, first_w, feed_width, first_saved)
    first_sums = [collect_grads(g) for g in first_grads]
    grad_one, first_gain_grad = norm_step(grad_two, stream_one, gains[1], plane_scatter(partial))
    second_cat = jnp.concatenate(second_sums, -1)
    grad_one, attend_sums, second_cat = together(grad_one, attend_sums, second_cat)

    grad_all = plane_gather(low(grad_one))
    mixer_out_grad = dot_tn(grad_all, conv_gated)
    gated_grad = dot_nn(grad_all, mixer_out_w).reshape(seqs, rows, channels)
    gate_c_grad = low(gated_grad * conv_sum)
    sum_grad = gated_grad * gate_c
    tap_rows = []
    spread = jnp.zeros_like(extended)
    for j in range(3):
        masked = sum_grad * in_doc[j]
        tap_rows.append(jnp.sum(masked * extended[:, 2 - j : 2 - j + rows], (0, 1)))
        spread = spread + jnp.pad(own_taps[j] * masked, ((0, 0), (2 - j, j), (0, 0)))
    spread, second_cat = together(spread, second_cat)
    returned = shifted(spread[:, :2], "ctx", -1)
    returned, *second_parts = together(returned, *send_back(second_cat))
    src_grad = spread[:, 2:] + jnp.pad(returned, ((0, 0), (rows - 2, 0), (0, 0)))
    proj_grad = jnp.concatenate(
        [low(src_grad * conv_input), gate_c_grad, low(src_grad * gate_b)], -1
    ).reshape(seqs * rows, 3 * channels)
    mixer_in_grad = dot_tn(mixer_norm, proj_grad)
    mixer_grads = low(jnp.concatenate([mixer_in_grad, mixer_out_grad], -1))
    mixer_grads = turn_blocks(
        mixer_grads.reshape(ctxs, seqs, part, 4 * channels).swapaxes(0, 1), 7
    ).reshape(ctxs, seqs * part, 4 * channels)
    proj_grad, mixer_grads = together(proj_grad, mixer_grads)
    mixer_sums = lax.psum_scatter(mixer_grads, "ctx", scatter_dimension=0, tiled=False)
    grad_zero, mixer_gain_grad = norm_step(
        grad_one,
        stream_zero,
        gains[0],
        plane_scatter(dot_nt(proj_grad, mixer_in_w)),
    )
    hidden_out = both_halves(stream_three + last_branch)
    hidden_grad = both_halves(grad_zero)

    gain_rows = restore(
        jnp.stack([mixer_gain_grad, first_gain_grad, attend_gain_grad, second_gain_grad])
    )
    taps_part = lax.dynamic_update_slice(
        jnp.zeros((tens, 3, channels * seqs), jnp.float32),
        jnp.stack(tap_rows)[None],
        (ten, 0, dp * channels),
    )
    small = jnp.concatenate(
        [gain_rows.reshape(-1), query_gain_part, key_gain_part, taps_part.reshape(-1)]
    )
    small = small_sum(small, 5)
    first_parts = send_back(jnp.concatenate(first_sums + [attend_sums], -1))
    hidden_grad, mixer_sums = together(hidden_grad, mixer_sums)
    mixer_done = wide(mixer_sums).reshape(seqs, part, -1).swapaxes(0, 1)
    gain_sums = lax.dynamic_slice_in_dim(
        small[: 4 * width].reshape(4, width), (dp * ctxs + ctx) * part, part, 1
    )
    query_gain_grad = small[4 * width : 4 * width + HD]
    key_gain_grad = small[4 * width + HD : 4 * width + 2 * HD]
    taps_grad = lax.dynamic_index_in_dim(
        small[4 * width + 2 * HD :].reshape(tens, 3, channels * seqs), ten, 0, keepdims=False
    )

    def columns(done, start, count):
        return done[:, :, start : start + count].reshape(part, -1)

    def feed_columns(parts, number):
        return by_source(parts, number * feed_width, feed_width)[:, :units]

    attend_at = 3 * feed_width

    return (
        hidden_out,
        hidden_grad,
        gain_sums[0],
        jnp.stack([columns(mixer_done, k * channels, channels) for k in range(3)]),
        taps_grad,
        columns(mixer_done, 3 * channels, channels).T,
        gain_sums[1],
        feed_columns(first_parts, 0),
        feed_columns(first_parts, 1),
        feed_columns(first_parts, 2).T,
        gain_sums[2],
        by_source(first_parts, attend_at, q_cols),
        by_source(first_parts, attend_at + q_cols, kv_cols),
        by_source(first_parts, attend_at + q_cols + kv_cols, kv_cols),
        query_gain_grad,
        key_gain_grad,
        by_source(first_parts, attend_at + q_cols + 2 * kv_cols, q_cols).T,
        gain_sums[3],
        feed_columns(second_parts, 0),
        feed_columns(second_parts, 1),
        feed_columns(second_parts, 2).T,
    )


def solution(mesh):
    rows = P("dp", "ctx", None)
    gain = P(("dp", "ctx"))
    into = P(("dp", "ctx"), "tensor")
    out = P("tensor", ("dp", "ctx"))
    thrice = P(None, ("dp", "ctx"), "tensor")
    taps = P(None, "tensor")
    weights = (
        (gain, thrice, taps, out, gain, into, into, out)
        + (gain, into, into, into, P(), P(), out)
        + (gain, into, into, out)
    )
    return jax.shard_map(
        shards,
        mesh=mesh,
        in_specs=(rows, P("dp", "ctx")) + weights + (rows,),
        out_specs=(rows, rows) + weights,
        check_vma=False,
    )
```

```python
import functools
import math

import jax
import jax.numpy as jnp
from jax import lax
from jax.experimental import pallas as pl
from jax.experimental.pallas import tpu as pltpu
from jax.sharding import PartitionSpec as P

H = 24
KV = 8
HD = 64
GROUPS = H // KV
LANES = 128

epsilon = 1e-05
MESH = pl.DeviceIdType.MESH


def plane_place():
    dp = lax.axis_index("dp")
    ten = lax.axis_index("tensor")
    core = lax.rem(dp, 2)
    across = lax.rem(dp + 2, 4)
    twin = dp + 1 - 2 * core
    return dp, ten, core, across, twin


def greet(dp, ten, across, twin):
    barrier = pltpu.get_barrier_semaphore()
    pl.semaphore_signal(barrier, 1, device_id={"dp": across}, device_id_type=MESH)
    pl.semaphore_signal(barrier, 1, device_id={"tensor": 1 - ten}, device_id_type=MESH)
    pl.semaphore_signal(barrier, 1, device_id={"dp": twin}, device_id_type=MESH)
    pl.semaphore_wait(barrier, 3)


def remote(src, dst, send, recv, place):
    return pltpu.make_async_remote_copy(
        src_ref=src,
        dst_ref=dst,
        send_sem=send,
        recv_sem=recv,
        device_id=place,
        device_id_type=MESH,
    )


def gather_kernel(x_ref, o_ref, own_sem, send, recv):
    dp, ten, core, across, twin = plane_place()
    greet(dp, ten, across, twin)
    to_across = {"dp": across, "tensor": ten}
    to_side = {"dp": dp, "tensor": 1 - ten}
    to_twin = {"dp": twin, "tensor": ten}
    own = dp * 2 + ten
    first = (across * (1 - core) + dp * core) * 2 + ten * (1 - core) + (1 - ten) * core
    other = (dp * (1 - core) + across * core) * 2 + (1 - ten) * (1 - core) + ten * core
    onward = {
        "dp": dp * (1 - core) + across * core,
        "tensor": (1 - ten) * (1 - core) + ten * core,
    }
    far = across * 2 + 1 - ten

    def move(src, slot, number, place):
        copy = remote(src, o_ref.at[slot], send.at[number], recv.at[slot], place)
        copy.start()
        return copy

    copies = [
        move(x_ref, own, 0, to_across),
        move(x_ref, own, 1, to_side),
        move(x_ref, own, 2, to_twin),
    ]
    local = pltpu.make_async_copy(x_ref, o_ref.at[own], own_sem)
    local.start()

    def arrived(slot):
        remote(x_ref, o_ref.at[slot], send.at[0], recv.at[slot], to_twin).wait_recv()

    arrived(first)
    copies.append(move(o_ref.at[first], first, 3, onward))
    copies.append(move(o_ref.at[first], first, 4, to_twin))
    arrived(other)
    copies.append(move(o_ref.at[other], other, 5, to_twin))
    arrived(far)
    copies.append(move(o_ref.at[far], far, 6, to_twin))
    twin_across = lax.rem(twin + 2, 4)
    for there in (twin, twin_across):
        for side in range(2):
            arrived(there * 2 + side)
    local.wait()
    for copy in copies:
        copy.wait_send()


def plane_gather(block):
    rows, width = block.shape
    slots = lax.axis_size("dp") * lax.axis_size("tensor")
    gathered = pl.pallas_call(
        gather_kernel,
        out_shape=jax.ShapeDtypeStruct((slots, rows, width), block.dtype),
        in_specs=[pl.BlockSpec(memory_space=pltpu.VMEM)],
        out_specs=pl.BlockSpec(memory_space=pl.ANY),
        scratch_shapes=[
            pltpu.SemaphoreType.DMA,
            pltpu.SemaphoreType.DMA((7,)),
            pltpu.SemaphoreType.DMA((8,)),
        ],
        compiler_params=pltpu.CompilerParams(
            collective_id=1, has_side_effects=True, vmem_limit_bytes=16 << 20
        ),
    )(block)
    return gathered.reshape(slots * rows, width)


def scatter_kernel(p_ref, o_ref, mine, theirs, out_box, in_box, load, send, recv):
    dp, ten, core, across, twin = plane_place()
    greet(dp, ten, across, twin)
    twin_across = lax.rem(twin + 2, 4)
    to_twin = {"dp": twin, "tensor": ten}
    sides = (ten, 1 - ten, ten, 1 - ten)
    home = (dp, dp, across, across)
    away = (twin, twin, twin_across, twin_across)
    order = (3, 1, 2, 0)
    loads = {}
    gifts = {}
    for rel in order:
        gifts[rel] = remote(
            p_ref.at[away[rel] * 2 + sides[rel]],
            theirs.at[rel],
            send.at[rel],
            recv.at[rel],
            to_twin,
        )
        gifts[rel].start()
        loads[rel] = pltpu.make_async_copy(
            p_ref.at[home[rel] * 2 + sides[rel]], mine.at[rel], load.at[rel]
        )
        loads[rel].start()
    direct = 1 + core
    relayed = 2 - core
    to_direct = {
        "dp": dp * (1 - core) + across * core,
        "tensor": (1 - ten) * (1 - core) + ten * core,
    }
    to_relayed = {
        "dp": across * (1 - core) + dp * core,
        "tensor": ten * (1 - core) + (1 - ten) * core,
    }

    def total(rel):
        return mine[rel].astype(jnp.float32) + theirs[rel].astype(jnp.float32)

    def post(number, value, place):
        out_box[number] = value.astype(out_box.dtype)
        copy = remote(
            out_box.at[number], in_box.at[number], send.at[4 + number], recv.at[4 + number], place
        )
        copy.start()
        return copy

    loads[3].wait()
    gifts[3].wait_recv()
    relay = post(0, total(3), to_direct)
    for rel in (1, 2):
        loads[rel].wait()
        gifts[rel].wait_recv()
    straight = post(1, total(direct), to_direct)
    relay.wait_recv()
    bent = post(2, total(relayed) + in_box[0].astype(jnp.float32), to_relayed)
    loads[0].wait()
    gifts[0].wait_recv()
    partial = total(0)
    straight.wait_recv()
    partial = partial + in_box[1].astype(jnp.float32)
    bent.wait_recv()
    o_ref[...] = partial + in_box[2].astype(jnp.float32)
    for rel in order:
        gifts[rel].wait_send()
    for copy in (relay, straight, bent):
        copy.wait_send()


def plane_scatter(partial):
    slots = lax.axis_size("dp") * lax.axis_size("tensor")
    rows, width = partial.shape[0] // slots, partial.shape[1]
    block = (rows, width)
    return pl.pallas_call(
        scatter_kernel,
        out_shape=jax.ShapeDtypeStruct(block, jnp.float32),
        in_specs=[pl.BlockSpec(memory_space=pl.ANY)],
        out_specs=pl.BlockSpec(memory_space=pltpu.VMEM),
        scratch_shapes=[
            pltpu.VMEM((4,) + block, jnp.bfloat16),
            pltpu.VMEM((4,) + block, jnp.bfloat16),
            pltpu.VMEM((3,) + block, jnp.bfloat16),
            pltpu.VMEM((3,) + block, jnp.bfloat16),
            pltpu.SemaphoreType.DMA((4,)),
            pltpu.SemaphoreType.DMA((7,)),
            pltpu.SemaphoreType.DMA((7,)),
        ],
        compiler_params=pltpu.CompilerParams(
            collective_id=2, has_side_effects=True, vmem_limit_bytes=24 << 20
        ),
    )(partial.astype(jnp.bfloat16).reshape((slots,) + block))


def swap_kernel(x_ref, o_ref, own_sem, send, recv):
    dp = lax.axis_index("dp")
    ten = lax.axis_index("tensor")
    barrier = pltpu.get_barrier_semaphore()
    for step in (1, 2, 3):
        pl.semaphore_signal(
            barrier,
            1,
            device_id={"dp": lax.rem(dp + step, 4), "tensor": ten},
            device_id_type=MESH,
        )
    pl.semaphore_wait(barrier, 3)
    copies = []
    for step in (2, 1, 3):
        there = lax.rem(dp + step, 4)
        copy = remote(
            x_ref.at[there],
            o_ref.at[dp],
            send.at[step],
            recv.at[step],
            {"dp": there, "tensor": ten},
        )
        copy.start()
        copies.append(copy)
    local = pltpu.make_async_copy(x_ref.at[dp], o_ref.at[dp], own_sem)
    local.start()
    for copy in copies:
        copy.wait()
    local.wait()


def turn_kernel(x_ref, o_ref, own_sem, send, recv):
    dp = lax.axis_index("dp")
    ten = lax.axis_index("tensor")
    barrier = pltpu.get_barrier_semaphore()
    for step in (1, 2, 3):
        pl.semaphore_signal(
            barrier,
            1,
            device_id={"dp": lax.rem(dp + step, 4), "tensor": ten},
            device_id_type=MESH,
        )
    pl.semaphore_wait(barrier, 3)
    copies = []
    for step in (2, 1, 3):
        there = lax.rem(dp + step, 4)
        copy = remote(
            x_ref.at[there],
            o_ref.at[:, dp],
            send.at[step],
            recv.at[step],
            {"dp": there, "tensor": ten},
        )
        copy.start()
        copies.append(copy)
    local = pltpu.make_async_copy(x_ref.at[dp], o_ref.at[:, dp], own_sem)
    local.start()
    for copy in copies:
        copy.wait()
    local.wait()


def turn_blocks(blocks, number):
    shape = (blocks.shape[1], blocks.shape[0]) + blocks.shape[2:]
    return pl.pallas_call(
        turn_kernel,
        out_shape=jax.ShapeDtypeStruct(shape, blocks.dtype),
        in_specs=[pl.BlockSpec(memory_space=pltpu.VMEM)],
        out_specs=pl.BlockSpec(memory_space=pl.ANY),
        scratch_shapes=[
            pltpu.SemaphoreType.DMA,
            pltpu.SemaphoreType.DMA((4,)),
            pltpu.SemaphoreType.DMA((4,)),
        ],
        compiler_params=pltpu.CompilerParams(
            collective_id=number, has_side_effects=True, vmem_limit_bytes=16 << 20
        ),
    )(blocks)


def swap_blocks(blocks, number):
    return pl.pallas_call(
        swap_kernel,
        out_shape=jax.ShapeDtypeStruct(blocks.shape, blocks.dtype),
        in_specs=[pl.BlockSpec(memory_space=pltpu.VMEM)],
        out_specs=pl.BlockSpec(memory_space=pl.ANY),
        scratch_shapes=[
            pltpu.SemaphoreType.DMA,
            pltpu.SemaphoreType.DMA((4,)),
            pltpu.SemaphoreType.DMA((4,)),
        ],
        compiler_params=pltpu.CompilerParams(
            collective_id=number, has_side_effects=True, vmem_limit_bytes=16 << 20
        ),
    )(blocks)


def send_back(blocks):
    dp = lax.axis_index("dp")
    devices = range(lax.axis_size("dp"))
    parts = [lax.dynamic_index_in_dim(blocks, dp, 0, keepdims=False)]
    for flip in (1, 2, 3):
        sent = lax.dynamic_index_in_dim(blocks, dp ^ flip, 0, keepdims=False)
        parts.append(lax.ppermute(sent, "dp", [(i, i ^ flip) for i in devices]))
    return parts


def by_source(parts, start, count):
    dp = lax.axis_index("dp")
    devices = range(lax.axis_size("dp"))
    cut = [part[:, start : start + count] for part in parts]
    return jnp.concatenate(
        [wide(lax.select_n(dp, *(cut[j ^ i] for i in devices))) for j in devices], 1
    )


def from_all_dp(block):
    dp = lax.axis_index("dp")
    devices = range(lax.axis_size("dp"))
    parts = [block] + [
        lax.ppermute(block, "dp", [(i, i ^ flip) for i in devices]) for flip in (1, 2, 3)
    ]
    return jnp.concatenate([lax.select_n(dp, *(parts[j ^ i] for i in devices)) for j in devices], 0)


def together(*values):
    return lax.optimization_barrier(values)


def small_sum_kernel(x_ref, o_ref, plane_box, plane_sum, line_box, send, recv, line_send, line_recv):
    dp, ten, ctx = (lax.axis_index(name) for name in ("dp", "tensor", "ctx"))
    dps, tens, ctxs = (lax.axis_size(name) for name in ("dp", "tensor", "ctx"))
    slots = dps * tens
    own = dp * tens + ten
    barrier = pltpu.get_barrier_semaphore()

    def plane_peer(step):
        slot = lax.rem(own + step, slots)
        return {"dp": slot // tens, "tensor": lax.rem(slot, tens), "ctx": ctx}

    def line_peer(step):
        return {"dp": dp, "tensor": ten, "ctx": lax.rem(ctx + step, ctxs)}

    for step in range(1, slots):
        pl.semaphore_signal(barrier, 1, device_id=plane_peer(step), device_id_type=MESH)
    for step in range(1, ctxs):
        pl.semaphore_signal(barrier, 1, device_id=line_peer(step), device_id_type=MESH)
    pl.semaphore_wait(barrier, slots + ctxs - 2)
    copies = []
    for step in range(1, slots):
        copy = remote(
            x_ref, plane_box.at[step], send.at[step], recv.at[step], plane_peer(step)
        )
        copy.start()
        copies.append(copy)
    total = x_ref[...]
    for copy in copies:
        copy.wait_recv()
    for step in range(1, slots):
        total = total + plane_box[step]
    plane_sum[...] = total
    lines = []
    for step in range(1, ctxs):
        copy = remote(
            plane_sum, line_box.at[step], line_send.at[step], line_recv.at[step], line_peer(step)
        )
        copy.start()
        lines.append(copy)
    for copy in lines:
        copy.wait_recv()
    for step in range(1, ctxs):
        total = total + line_box[step]
    o_ref[...] = total
    for copy in copies + lines:
        copy.wait_send()


def small_gather_kernel(x_ref, o_ref, own_sem, send, recv, line_send, line_recv):
    dp, ten, ctx = (lax.axis_index(name) for name in ("dp", "tensor", "ctx"))
    dps, ctxs = (lax.axis_size(name) for name in ("dp", "ctx"))
    barrier = pltpu.get_barrier_semaphore()

    def dp_peer(step):
        return {"dp": lax.rem(dp + step, dps), "tensor": ten, "ctx": ctx}

    def ctx_peer(step):
        return {"dp": dp, "tensor": ten, "ctx": lax.rem(ctx + step, ctxs)}

    for step in range(1, dps):
        pl.semaphore_signal(barrier, 1, device_id=dp_peer(step), device_id_type=MESH)
    for step in range(1, ctxs):
        pl.semaphore_signal(barrier, 1, device_id=ctx_peer(step), device_id_type=MESH)
    pl.semaphore_wait(barrier, dps + ctxs - 2)
    copies = []
    for step in range(1, dps):
        copy = remote(x_ref, o_ref.at[ctx, dp], send.at[step], recv.at[step], dp_peer(step))
        copy.start()
        copies.append(copy)
    local = pltpu.make_async_copy(x_ref, o_ref.at[ctx, dp], own_sem)
    local.start()
    local.wait()
    for copy in copies:
        copy.wait()
    lines = []
    for step in range(1, ctxs):
        copy = remote(
            o_ref.at[ctx], o_ref.at[ctx], line_send.at[step], line_recv.at[step], ctx_peer(step)
        )
        copy.start()
        lines.append(copy)
    for copy in lines:
        copy.wait()


def small_gather(block, number):
    dps, ctxs = lax.axis_size("dp"), lax.axis_size("ctx")
    return pl.pallas_call(
        small_gather_kernel,
        out_shape=jax.ShapeDtypeStruct((ctxs, dps) + block.shape, block.dtype),
        in_specs=[pl.BlockSpec(memory_space=pltpu.VMEM)],
        out_specs=pl.BlockSpec(memory_space=pltpu.VMEM),
        scratch_shapes=[
            pltpu.SemaphoreType.DMA,
            pltpu.SemaphoreType.DMA((dps,)),
            pltpu.SemaphoreType.DMA((dps,)),
            pltpu.SemaphoreType.DMA((ctxs,)),
            pltpu.SemaphoreType.DMA((ctxs,)),
        ],
        compiler_params=pltpu.CompilerParams(
            collective_id=number, has_side_effects=True, vmem_limit_bytes=16 << 20
        ),
    )(block)


def small_sum(values, number):
    count = values.size
    rows = -(-count // (8 * LANES)) * 8
    block = jnp.pad(values.reshape(-1), (0, rows * LANES - count)).reshape(rows, LANES)
    slots = lax.axis_size("dp") * lax.axis_size("tensor")
    ctxs = lax.axis_size("ctx")
    total = pl.pallas_call(
        small_sum_kernel,
        out_shape=jax.ShapeDtypeStruct(block.shape, jnp.float32),
        in_specs=[pl.BlockSpec(memory_space=pltpu.VMEM)],
        out_specs=pl.BlockSpec(memory_space=pltpu.VMEM),
        scratch_shapes=[
            pltpu.VMEM((slots,) + block.shape, jnp.float32),
            pltpu.VMEM(block.shape, jnp.float32),
            pltpu.VMEM((ctxs,) + block.shape, jnp.float32),
            pltpu.SemaphoreType.DMA((slots,)),
            pltpu.SemaphoreType.DMA((slots,)),
            pltpu.SemaphoreType.DMA((ctxs,)),
            pltpu.SemaphoreType.DMA((ctxs,)),
        ],
        compiler_params=pltpu.CompilerParams(
            collective_id=number, has_side_effects=True, vmem_limit_bytes=16 << 20
        ),
    )(block)
    return total.reshape(-1)[:count]


def rms_scale(values):
    return lax.rsqrt(jnp.mean(values * values, -1, keepdims=True) + epsilon)


def rms_back(values, upstream):
    row_scale = rms_scale(values)
    normed = values * row_scale
    return row_scale * (upstream - normed * jnp.mean(upstream * normed, -1, keepdims=True))


def low(values):
    return values.astype(jnp.bfloat16)


def wide(values):
    return values.astype(jnp.float32)


def dot_nn(left, right):
    return lax.dot_general(left, right, (((1,), (0,)), ((), ())), preferred_element_type=jnp.float32)


def dot_nt(left, right):
    return lax.dot_general(left, right, (((1,), (1,)), ((), ())), preferred_element_type=jnp.float32)


def dot_tn(left, right):
    return lax.dot_general(left, right, (((0,), (0,)), ((), ())), preferred_element_type=jnp.float32)


def shifted(block, axis, distance):
    devices = range(lax.axis_size(axis))
    route = [(i - distance, i) for i in devices if i - distance in devices]
    return lax.ppermute(block, axis, route)


def rotary_tables(positions, head_dim):
    half_dim = head_dim // 2
    freqs = jnp.exp(-math.log(1000000.0) * 2.0 * jnp.arange(half_dim, dtype=jnp.float32) / head_dim)
    angles = wide(positions)[..., None] * freqs
    return (jnp.cos(angles), jnp.sin(angles))


def rotate(values, cosine, sine):
    half_dim = values.shape[-1] // 2
    first, second = values[..., :half_dim], values[..., half_dim:]
    return jnp.concatenate([first * cosine - second * sine, second * cosine + first * sine], -1)


def visible(pos_ref, rows, key_rows):
    query_at = lax.broadcasted_iota(jnp.int32, (rows, key_rows), 0) + (key_rows - rows)
    key_at = lax.broadcasted_iota(jnp.int32, (rows, key_rows), 1)
    return (key_at <= query_at) & (key_at >= query_at - pos_ref[0])


def attend_kernel(q_ref, kv_ref, pos_ref, context_ref, lse_ref):
    rows = q_ref.shape[1]
    key_rows = kv_ref.shape[0] * rows
    both = kv_ref[...].reshape(key_rows, 2 * HD)
    keys, values = both[:, :HD], both[:, HD:]
    allowed = visible(pos_ref, rows, key_rows)
    contexts, totals = [], []
    for head in range(GROUPS):
        query = q_ref[0, :, head * HD : (head + 1) * HD]
        scores = jnp.where(allowed, dot_nt(query, keys) * (1.0 / math.sqrt(HD)), -1e30)
        top = jnp.max(scores, -1, keepdims=True)
        weights = jnp.exp(scores - top)
        total = jnp.sum(weights, -1, keepdims=True)
        contexts.append(low(dot_nn(low(weights * (1.0 / total)), values)))
        totals.append(top + jnp.log(total))
    context_ref[0] = jnp.concatenate(contexts, -1)
    lse_ref[0] = jnp.concatenate(totals + [jnp.zeros_like(totals[0])] * (8 - GROUPS), -1)


def attend_back_kernel(q_ref, kv_ref, pos_ref, lse_ref, grad_ref, dq_ref, dkv_ref):
    rows = q_ref.shape[1]
    key_rows = kv_ref.shape[0] * rows
    both = kv_ref[...].reshape(key_rows, 2 * HD)
    keys, values = both[:, :HD], both[:, HD:]
    allowed = visible(pos_ref, rows, key_rows)
    root = 1.0 / math.sqrt(HD)
    query_grads = []
    key_grad = jnp.zeros((key_rows, HD), jnp.float32)
    value_grad = jnp.zeros((key_rows, HD), jnp.float32)
    for head in range(GROUPS):
        query = q_ref[0, :, head * HD : (head + 1) * HD]
        grad = grad_ref[0, :, head * HD : (head + 1) * HD]
        scores = dot_nt(query, keys) * root - lse_ref[0, :, head : head + 1]
        probs = jnp.where(allowed, jnp.exp(jnp.where(allowed, scores, 0.0)), 0.0)
        prob_grad = dot_nt(grad, values)
        delta = jnp.sum(probs * prob_grad, -1, keepdims=True)
        score_grad = low(probs * (prob_grad - delta))
        query_grads.append(dot_nn(score_grad, keys) * root)
        key_grad = key_grad + dot_tn(score_grad, query)
        value_grad = value_grad + dot_tn(low(probs), grad)
    dq_ref[0] = jnp.concatenate(query_grads, -1)
    whole = low(jnp.concatenate([key_grad * root, value_grad], -1))
    dkv_ref[...] = whole.reshape(dkv_ref.shape)


def attend_specs(seqs, rows, parts):
    by_seq = lambda width: pl.BlockSpec((1, rows, width), lambda s: (s, 0, 0))
    over_keys = pl.BlockSpec((parts, 1, rows, 2 * HD), lambda s: (0, s, 0, 0))
    return by_seq, over_keys


def attend(queries, kv_all, positions):
    seqs, rows, width = queries.shape
    by_seq, over_keys = attend_specs(seqs, rows, kv_all.shape[0])
    return pl.pallas_call(
        attend_kernel,
        grid=(seqs,),
        out_shape=(
            jax.ShapeDtypeStruct(queries.shape, jnp.bfloat16),
            jax.ShapeDtypeStruct((seqs, rows, 8), jnp.float32),
        ),
        in_specs=[by_seq(width), over_keys, by_seq(1)],
        out_specs=(by_seq(width), by_seq(8)),
        compiler_params=pltpu.CompilerParams(vmem_limit_bytes=56 << 20),
    )(queries, kv_all, positions[..., None])


def attend_back(queries, kv_all, positions, totals, grads):
    seqs, rows, width = queries.shape
    by_seq, over_keys = attend_specs(seqs, rows, kv_all.shape[0])
    return pl.pallas_call(
        attend_back_kernel,
        grid=(seqs,),
        out_shape=(
            jax.ShapeDtypeStruct(queries.shape, jnp.float32),
            jax.ShapeDtypeStruct(kv_all.shape, jnp.bfloat16),
        ),
        in_specs=[by_seq(width), over_keys, by_seq(1), by_seq(8), by_seq(width)],
        out_specs=(by_seq(width), over_keys),
        compiler_params=pltpu.CompilerParams(vmem_limit_bytes=56 << 20),
    )(queries, kv_all, positions[..., None], totals, grads)


def column_blocks(weight, count, width):
    rows, columns = weight.shape
    weight = jnp.pad(weight, ((0, 0), (0, count * width - columns)))
    return weight.reshape(rows, count, width).transpose(1, 0, 2)


def spread_weights(blocks, number):
    mine = swap_blocks(blocks, number)
    whole = lax.all_gather(mine, "ctx", axis=0, tiled=False)
    return whole.reshape(-1, whole.shape[-1])


def collect_grads(grad):
    ctx, count = lax.axis_size("ctx"), lax.axis_size("dp")
    grad = low(grad).reshape(ctx, -1, grad.shape[-1])
    summed = lax.psum_scatter(grad, "ctx", scatter_dimension=0, tiled=False)
    return summed.reshape(count, -1, summed.shape[-1])


def feed_hidden(normed, weights, width):
    both = dot_nn(normed, weights[:, : 2 * width])
    gate, lift = both[:, :width], both[:, width:]
    return gate, lift, low(jax.nn.silu(gate) * lift)


def feed_down(hidden, weights, width):
    return low(dot_nt(hidden, weights[:, 2 * width :]))


def feed_backward(grad_all, normed, weights, width, saved):
    gate, lift, hidden = saved
    down_grad, grad_all = together(low(dot_tn(grad_all, hidden)), grad_all)
    hidden_grad = dot_nn(grad_all, weights[:, 2 * width :])
    sig = jax.nn.sigmoid(gate)
    gate_grad = low(hidden_grad * lift * sig * (1.0 + gate * (1.0 - sig)))
    lift_grad = low(hidden_grad * gate * sig)
    gate_weight_grad = low(dot_tn(normed, gate_grad))
    lift_weight_grad = low(dot_tn(normed, lift_grad))
    gate_grad, lift_grad, gate_weight_grad, lift_weight_grad = together(
        gate_grad, lift_grad, gate_weight_grad, lift_weight_grad
    )
    partial = dot_nt(gate_grad, weights[:, :width]) + dot_nt(
        lift_grad, weights[:, width : 2 * width]
    )
    return partial, (gate_weight_grad, lift_weight_grad, down_grad)


def shards(
    hidden_in,
    doc_pos,
    mixer_gain,
    mixer_in,
    conv_taps,
    mixer_out,
    feed_first,
    gate_first,
    lift_first,
    down_first,
    attend_gain,
    query_proj,
    key_proj,
    value_proj,
    query_gain,
    key_gain,
    attend_out,
    feed_second,
    gate_second,
    lift_second,
    down_second,
    output_grad,
):
    dp, ten, ctx = (lax.axis_index(name) for name in ("dp", "tensor", "ctx"))
    seqs, tens, ctxs = (lax.axis_size(name) for name in ("dp", "tensor", "ctx"))
    rows, width = hidden_in.shape[1], hidden_in.shape[2]
    own_rows = rows // tens
    part = mixer_gain.shape[0]
    channels = mixer_in.shape[2] // seqs
    units = gate_first.shape[1]
    feed_width = -(-units // (seqs * LANES)) * LANES

    def regroup(values):
        lead = values.shape[:-1]
        return values.reshape(lead + (seqs, ctxs, part)).swapaxes(-3, -2).reshape(lead + (width,))

    def restore(values):
        lead = values.shape[:-1]
        return values.reshape(lead + (ctxs, seqs, part)).swapaxes(-3, -2).reshape(lead + (width,))

    def own_half(values):
        return regroup(lax.dynamic_slice_in_dim(values[0], ten * own_rows, own_rows, 0))

    stream_zero = wide(own_half(hidden_in))
    upstream = wide(own_half(output_grad))
    last_grad_all = plane_gather(low(upstream))

    def norm_rows(stream, gain):
        return low(stream * rms_scale(stream) * gain)

    mixer_blocks = jnp.concatenate(
        [column_blocks(mixer_in[k], seqs, channels) for k in range(3)]
        + [column_blocks(mixer_out.T, seqs, channels)],
        -1,
    )
    mixer_w = spread_weights(mixer_blocks, 3)
    own_gains = wide(jnp.stack([mixer_gain, feed_first, attend_gain, feed_second]))
    own_gains = jnp.pad(own_gains, ((0, 4), (0, -part % LANES)))
    gains = small_gather(own_gains, 8)[:, :, :4, :part]
    gains = gains.transpose(2, 0, 1, 3).reshape(4, width)
    first_blocks = jnp.concatenate(
        [column_blocks(w, seqs, feed_width) for w in (gate_first, lift_first, down_first.T)], -1
    )
    first_w = spread_weights(first_blocks, 4)
    q_cols, kv_cols = query_proj.shape[1] // seqs, key_proj.shape[1] // seqs
    attend_blocks = jnp.concatenate(
        [
            column_blocks(query_proj, seqs, q_cols),
            column_blocks(key_proj, seqs, kv_cols),
            column_blocks(value_proj, seqs, kv_cols),
            column_blocks(attend_out.T, seqs, q_cols),
        ],
        -1,
    )
    attend_w = spread_weights(attend_blocks, 6)
    second_blocks = jnp.concatenate(
        [column_blocks(w, seqs, feed_width) for w in (gate_second, lift_second, down_second.T)], -1
    )
    second_w = spread_weights(second_blocks, 4)

    positions = from_all_dp(doc_pos)
    mixer_norm = plane_gather(norm_rows(stream_zero, gains[0]))
    mixer_w, mixer_norm, last_grad_all = together(mixer_w, mixer_norm, last_grad_all)
    own_taps = wide(lax.dynamic_slice_in_dim(conv_taps, dp * channels, channels, 1))

    mixer_in_w, mixer_out_w = mixer_w[:, : 3 * channels], mixer_w[:, 3 * channels : 4 * channels]
    projected = dot_nn(mixer_norm, mixer_in_w).reshape(seqs, rows, 3 * channels)
    gate_b = projected[..., :channels]
    gate_c = projected[..., channels : 2 * channels]
    conv_input = projected[..., 2 * channels :]
    conv_src = low(gate_b * conv_input)
    earlier = shifted(conv_src[:, -2:], "ctx", 1)
    extended = wide(jnp.concatenate([earlier, conv_src], 1))
    in_doc = [wide(positions >= offset)[..., None] for offset in range(3)]
    conv_sum = sum(
        own_taps[j] * extended[:, 2 - j : 2 - j + rows] * in_doc[j] for j in range(3)
    )
    conv_gated = low(gate_c * conv_sum).reshape(seqs * rows, channels)
    stream_one = stream_zero + plane_scatter(dot_nt(conv_gated, mixer_out_w))

    first_norm = plane_gather(norm_rows(stream_one, gains[1]))
    first_saved = feed_hidden(first_norm, first_w, feed_width)
    stream_two = stream_one + plane_scatter(feed_down(first_saved[2], first_w, feed_width))

    attend_norm = plane_gather(norm_rows(stream_two, gains[2]))
    qkv_w = attend_w[:, : q_cols + 2 * kv_cols]
    attend_out_w = attend_w[:, q_cols + 2 * kv_cols :]
    qkv = dot_nn(attend_norm, qkv_w).reshape(seqs, rows, -1)
    queries = qkv[..., :q_cols].reshape(seqs, rows, -1, HD)
    keys = qkv[..., q_cols : q_cols + kv_cols].reshape(seqs, rows, -1, HD)
    values = qkv[..., q_cols + kv_cols :].reshape(seqs, rows, -1, HD)
    cosine, sine = (table[:, :, None] for table in rotary_tables(positions, HD))
    query_scale, key_scale = rms_scale(queries), rms_scale(keys)
    q_gain, k_gain = wide(query_gain), wide(key_gain)
    query_rot = low(rotate(queries * query_scale * q_gain, cosine, sine))
    key_rot = low(rotate(keys * key_scale * k_gain, cosine, sine))
    kv_own = jnp.concatenate([key_rot, low(values)], -1).reshape(seqs, rows, 2 * HD)
    kv_all = jnp.stack(
        [shifted(kv_own, "ctx", distance) for distance in range(ctxs - 1, 0, -1)] + [kv_own]
    )
    query_rows = query_rot.reshape(seqs, rows, q_cols)
    context, totals = attend(query_rows, kv_all, positions)
    context = context.reshape(seqs * rows, q_cols)
    stream_three = stream_two + plane_scatter(dot_nt(context, attend_out_w))

    second_norm = plane_gather(norm_rows(stream_three, gains[3]))
    second_saved = feed_hidden(second_norm, second_w, feed_width)

    def both_halves(values):
        values = low(restore(values))
        other = lax.ppermute(values, "tensor", [(i, 1 - i) for i in range(tens)])
        lower = lax.select_n(ten, values, other)
        upper = lax.select_n(ten, other, values)
        return jnp.concatenate([lower, upper], 0)[None]

    def norm_step(upstream, stream, gain, normed_grad):
        gain_grad = jnp.sum(normed_grad * stream * rms_scale(stream), 0)
        return upstream + rms_back(stream, normed_grad * gain), gain_grad

    partial, second_grads = feed_backward(last_grad_all, second_norm, second_w, feed_width, second_saved)
    second_sums = [collect_grads(g) for g in second_grads]
    grad_three, second_gain_grad = norm_step(
        upstream, stream_three, gains[3], plane_scatter(partial)
    )

    grad_all = plane_gather(low(grad_three))
    grad_all, second_sums[2] = together(grad_all, second_sums[2])
    attend_out_grad = dot_tn(grad_all, context)
    context_grad = low(dot_nn(grad_all, attend_out_w)).reshape(seqs, rows, q_cols)
    query_acc, kv_acc = attend_back(query_rows, kv_all, positions, totals, context_grad)
    query_acc = query_acc.reshape(seqs, rows, -1, HD)
    late_hidden, kv_acc = together(second_saved[2], kv_acc)
    kv_sent = [
        shifted(kv_acc[ctxs - 1 - distance], "ctx", -distance) for distance in range(1, ctxs)
    ]
    last_branch = plane_scatter(feed_down(late_hidden, second_w, feed_width))
    last_branch, *kv_sent = together(last_branch, *kv_sent)
    kv_mine = wide(kv_acc[ctxs - 1]) + sum(wide(sent) for sent in kv_sent)
    key_grads, value_grads = kv_mine[..., :HD], kv_mine[..., HD:]
    query_norm_grad = rotate(query_acc, cosine, -sine)
    key_norm_grad = rotate(key_grads[:, :, None], cosine, -sine)
    query_gain_part = jnp.sum(query_norm_grad * queries * query_scale, (0, 1, 2))
    key_gain_part = jnp.sum(key_norm_grad * keys * key_scale, (0, 1, 2))
    query_grad = low(rms_back(queries, query_norm_grad * q_gain)).reshape(seqs * rows, -1)
    key_grad = low(rms_back(keys, key_norm_grad * k_gain)).reshape(seqs * rows, -1)
    value_grad = low(value_grads).reshape(seqs * rows, -1)
    qkv_grad = jnp.concatenate([query_grad, key_grad, value_grad], -1)
    qkv_weight_grad = dot_tn(attend_norm, qkv_grad)
    attend_grads = low(jnp.concatenate([qkv_weight_grad, attend_out_grad], -1))
    qkv_grad, attend_grads = together(qkv_grad, attend_grads)
    attend_sums = collect_grads(attend_grads)
    grad_two, attend_gain_grad = norm_step(
        grad_three,
        stream_two,
        gains[2],
        plane_scatter(dot_nt(qkv_grad, qkv_w)),
    )
    grad_two, *second_sums = together(grad_two, *second_sums)

    grad_all = plane_gather(low(grad_two))
    partial, first_grads = feed_backward(grad_all, first_norm, first_w, feed_width, first_saved)
    first_sums = [collect_grads(g) for g in first_grads]
    grad_one, first_gain_grad = norm_step(grad_two, stream_one, gains[1], plane_scatter(partial))
    second_cat = jnp.concatenate(second_sums, -1)
    grad_one, attend_sums, second_cat = together(grad_one, attend_sums, second_cat)

    grad_all = plane_gather(low(grad_one))
    mixer_out_grad = dot_tn(grad_all, conv_gated)
    gated_grad = dot_nn(grad_all, mixer_out_w).reshape(seqs, rows, channels)
    gate_c_grad = low(gated_grad * conv_sum)
    sum_grad = gated_grad * gate_c
    tap_rows = []
    spread = jnp.zeros_like(extended)
    for j in range(3):
        masked = sum_grad * in_doc[j]
        tap_rows.append(jnp.sum(masked * extended[:, 2 - j : 2 - j + rows], (0, 1)))
        spread = spread + jnp.pad(own_taps[j] * masked, ((0, 0), (2 - j, j), (0, 0)))
    spread, second_cat = together(spread, second_cat)
    returned = shifted(spread[:, :2], "ctx", -1)
    returned, *second_parts = together(returned, *send_back(second_cat))
    src_grad = spread[:, 2:] + jnp.pad(returned, ((0, 0), (rows - 2, 0), (0, 0)))
    proj_grad = jnp.concatenate(
        [low(src_grad * conv_input), gate_c_grad, low(src_grad * gate_b)], -1
    ).reshape(seqs * rows, 3 * channels)
    mixer_in_grad = dot_tn(mixer_norm, proj_grad)
    mixer_grads = low(jnp.concatenate([mixer_in_grad, mixer_out_grad], -1))
    mixer_grads = turn_blocks(
        mixer_grads.reshape(ctxs, seqs, part, 4 * channels).swapaxes(0, 1), 7
    ).reshape(ctxs, seqs * part, 4 * channels)
    proj_grad, mixer_grads = together(proj_grad, mixer_grads)
    mixer_sums = lax.psum_scatter(mixer_grads, "ctx", scatter_dimension=0, tiled=False)
    grad_zero, mixer_gain_grad = norm_step(
        grad_one,
        stream_zero,
        gains[0],
        plane_scatter(dot_nt(proj_grad, mixer_in_w)),
    )
    hidden_out = both_halves(stream_three + last_branch)
    hidden_grad = both_halves(grad_zero)

    gain_rows = restore(
        jnp.stack([mixer_gain_grad, first_gain_grad, attend_gain_grad, second_gain_grad])
    )
    taps_part = lax.dynamic_update_slice(
        jnp.zeros((tens, 3, channels * seqs), jnp.float32),
        jnp.stack(tap_rows)[None],
        (ten, 0, dp * channels),
    )
    small = jnp.concatenate(
        [gain_rows.reshape(-1), query_gain_part, key_gain_part, taps_part.reshape(-1)]
    )
    small, mixer_sums = together(small, mixer_sums)
    small = small_sum(small, 5)
    first_parts = send_back(jnp.concatenate(first_sums + [attend_sums], -1))
    mixer_sums = mixer_sums.reshape(seqs, part, -1)
    gain_sums = lax.dynamic_slice_in_dim(
        small[: 4 * width].reshape(4, width), (dp * ctxs + ctx) * part, part, 1
    )
    query_gain_grad = small[4 * width : 4 * width + HD]
    key_gain_grad = small[4 * width + HD : 4 * width + 2 * HD]
    taps_grad = lax.dynamic_index_in_dim(
        small[4 * width + 2 * HD :].reshape(tens, 3, channels * seqs), ten, 0, keepdims=False
    )

    def mixer_columns(number):
        cut = mixer_sums[:, :, number * channels : (number + 1) * channels]
        return jnp.concatenate([wide(cut[j]) for j in range(seqs)], 1)

    def feed_columns(parts, number):
        return by_source(parts, number * feed_width, feed_width)[:, :units]

    attend_at = 3 * feed_width

    return (
        hidden_out,
        hidden_grad,
        gain_sums[0],
        jnp.stack([mixer_columns(k) for k in range(3)]),
        taps_grad,
        mixer_columns(3).T,
        gain_sums[1],
        feed_columns(first_parts, 0),
        feed_columns(first_parts, 1),
        feed_columns(first_parts, 2).T,
        gain_sums[2],
        by_source(first_parts, attend_at, q_cols),
        by_source(first_parts, attend_at + q_cols, kv_cols),
        by_source(first_parts, attend_at + q_cols + kv_cols, kv_cols),
        query_gain_grad,
        key_gain_grad,
        by_source(first_parts, attend_at + q_cols + 2 * kv_cols, q_cols).T,
        gain_sums[3],
        feed_columns(second_parts, 0),
        feed_columns(second_parts, 1),
        feed_columns(second_parts, 2).T,
    )


def solution(mesh):
    rows = P("dp", "ctx", None)
    gain = P(("dp", "ctx"))
    into = P(("dp", "ctx"), "tensor")
    out = P("tensor", ("dp", "ctx"))
    thrice = P(None, ("dp", "ctx"), "tensor")
    taps = P(None, "tensor")
    weights = (
        (gain, thrice, taps, out, gain, into, into, out)
        + (gain, into, into, into, P(), P(), out)
        + (gain, into, into, out)
    )
    return jax.shard_map(
        shards,
        mesh=mesh,
        in_specs=(rows, P("dp", "ctx")) + weights + (rows,),
        out_specs=(rows, rows) + weights,
        check_vma=False,
    )
```
